32 devices in a mesh: band: 8 (over z, x), lev: 4 (over y, core).
Axes of the slice: x: 2, y: 2, z: 4, core: 2. Of those that a mesh axis runs over, the one named last changes fastest.
Arguments:
- temp_spectrum: bfloat16 [160, 1280, 2, 136], P('band', None, None, 'lev'), may hold values from -0.875 to 0.875
- surf_spectrum: bfloat16 [160, 1280, 2], P('band'), may hold values from -0.875 to 0.875
- legendre: bfloat16 [160, 16, 1280], P('band'), may hold values from -0.15625 to 0.15625
- m_order: int32 [160], replicated, may hold values from 0 to 159, each once
- hydro_matrix: bfloat16 [136, 136], P('lev'), may hold values from 0.029907227 to 0.29882812
- surf_coupling: float32 [136], P('lev'), may hold values from 0.3 to 3
- src_blocks: int32 [640, 4], P('band'), may hold values from 0 to 639, as said below
- tap_index: int32 [640, 4, 128], P('band'), may hold values from 0 to 511
- tap_weight: float32 [640, 4, 128], P('band'), may hold values from 0.05 to 0.45
Outputs:
- departed: float32 [16, 136, 5120], P('band', 'lev')
The draws below stay inside these ranges and needn't reach their ends.
Inputs may be any that keep to these rules, and one draw needn't show every extreme that they name: `src_blocks`: slots 0 and 2 of a reader block name blocks of the reader's own band device, slot 1 a block of the device before it and slot 3 a block of the device after it, or of the reader's own device where that neighbour does not exist. The readers of one device name at most 16 distinct blocks of each neighbour, and some device names exactly 16 of one neighbour.
All inputs are finite; a program needn't handle non-finite values.
Results may differ from the reference program's by a relative error of at most 0.0047.
Values may be sent and summed in bfloat16 or wider, within the bound.
A program may use at most 128 MiB of HBM per device.

```python
import math
import jax
import jax.numpy as jnp
from jax import lax

NN = 1280
LEV = 136
NLON = 5120
BLK = 128
SLOTS = 4
TAPS = 4
CAP = 16
LAT_DEV = 2
MM = 160
LAT = 16
NB = 640


def draw_src_blocks(key, part):
    per_device = LAT_DEV * NLON // BLK
    band_count = NB // per_device
    key_list = jax.random.split(key, 4)
    reader = jnp.arange(NB, dtype=jnp.int32)
    device_of = reader // per_device
    local_idx = reader % per_device
    own_first = device_of * per_device + jax.random.randint(key_list[0], (NB,), 0, per_device)
    own_second = device_of * per_device + jax.random.randint(key_list[1], (NB,), 0, per_device)

    def one_side(side_key, offset):
        key_counts, key_forced, key_order, key_spare = jax.random.split(side_key, 4)
        counts = jax.random.randint(key_counts, (band_count,), max(1, CAP // 4), CAP + 1)
        forced = jax.random.randint(key_forced, (), 0, band_count - 1)
        forced_device = jnp.where(offset < 0, forced + 1, forced)
        counts = counts.at[forced_device].set(CAP)
        orderings = jax.vmap(lambda sub_key: jax.random.permutation(sub_key, per_device))(jax.random.split(key_order, band_count))
        neighbour = device_of + offset
        exists = (neighbour >= 0) & (neighbour < band_count)
        chosen = orderings[device_of, local_idx % counts[device_of]].astype(jnp.int32)
        spare = device_of * per_device + jax.random.randint(key_spare, (NB,), 0, per_device)
        return jnp.where(exists, neighbour * per_device + chosen, spare).astype(jnp.int32)
    from_before = one_side(key_list[2], -1)
    from_after = one_side(key_list[3], 1)
    return jnp.stack([own_first, from_before, own_second, from_after], axis=1).astype(jnp.int32)


def plant(entries, own_key, low, high):
    spot = [jax.random.randint(jax.random.fold_in(own_key, axis), (), 0, length) for axis, length in enumerate(entries.shape)]
    longest = entries.shape.index(max(entries.shape))
    beside = spot[:longest] + [(spot[longest] + 1) % entries.shape[longest]] + spot[longest + 1:]
    return entries.at[tuple(spot)].set(low).at[tuple(beside)].set(high)


def levels(stream_key, extent, shards, smallest, high):
    gain = 1.0
    for position, parts in shards:
        heights = jax.random.uniform(jax.random.fold_in(jax.random.fold_in(stream_key, 6), position), (parts,), jnp.float32, smallest / len(shards), high / len(shards))
        gain = gain * jnp.repeat(jnp.exp(heights), extent[position] // parts).reshape((-1,) + (1,) * (len(extent) - 1 - position))
    return gain


def noise(stream_key, extent, width, bound, pieces=(), kind=jnp.bfloat16):
    array = width * jax.random.normal(stream_key, extent, jnp.float32)
    if pieces:
        array = array * levels(stream_key, extent, pieces, -0.22, 0.18)
    return jnp.clip(array, -bound, bound).astype(kind)


def setup_inputs(seed: int = 0) -> dict:
    arg_keys = jax.random.split(jax.random.key(seed), 10)
    return {
        "temp_spectrum": noise(arg_keys[0], (MM, NN, 2, LEV), ((2 * MM) ** -0.5), 0.875, ((0, 8), (3, 4))),
        "surf_spectrum": noise(arg_keys[1], (MM, NN, 2), ((2 * MM) ** -0.5), 0.875, ((0, 8),)),
        "legendre": noise(arg_keys[2], (MM, LAT, NN), NN ** -0.5, 0.15625, ((0, 8),)),
        "m_order": jax.random.permutation(arg_keys[3], MM).astype(jnp.int32),
        "hydro_matrix": jnp.clip(jnp.exp(math.log(0.29882812) - 2.30176843 * jax.random.uniform(arg_keys[4], (LEV, LEV), jnp.float32) ** levels(arg_keys[4], (LEV, LEV), ((0, 4),), -0.2, 0.2)), 0.029907227, 0.29882812).astype(jnp.bfloat16),
        "surf_coupling": jnp.clip(jnp.exp(math.log(3.0) - 2.3025851 * jax.random.uniform(arg_keys[5], (LEV,), jnp.float32) ** levels(arg_keys[5], (LEV,), ((0, 4),), -0.2, 0.2)), 0.3, 3.0),
        "src_blocks": draw_src_blocks(jax.random.fold_in(arg_keys[9], 71), 0),
        "tap_index": plant(jax.random.randint(arg_keys[7], (NB, TAPS, BLK), 0, SLOTS * BLK), jax.random.fold_in(arg_keys[7], 1), 0, (SLOTS * BLK) - 1).astype(jnp.int32),
        "tap_weight": jnp.clip(0.05 + 0.39999999 * jax.random.uniform(arg_keys[8], (NB, TAPS, BLK), jnp.float32) ** levels(arg_keys[8], (NB, TAPS, BLK), ((0, 8),), -0.2, 0.2), 0.05, 0.45),
    }


def synth_table(m_values, nlon):
    columns = lax.broadcasted_iota(jnp.int32, (m_values.shape[0], nlon), 1)
    phase = (m_values[:, None] * columns) % nlon
    angle = phase.astype(jnp.float32) * (2.0 * math.pi / nlon)
    factor = jnp.where(m_values == 0, 1.0, 2.0).astype(jnp.float32)[:, None]
    return jnp.stack([factor * jnp.cos(angle), -factor * jnp.sin(angle)], axis=1).astype(jnp.bfloat16)


def reference(temp_spectrum, surf_spectrum, legendre, m_order, hydro_matrix, surf_coupling, src_blocks, tap_index, tap_weight):
    n_index = jnp.arange(NN, dtype=jnp.int32)
    keep = n_index[None, :] >= m_order[:, None]
    masked_t = jnp.where(keep[:, :, None, None], temp_spectrum, jnp.zeros_like(temp_spectrum))
    masked_p = jnp.where(keep[:, :, None], surf_spectrum, jnp.zeros_like(surf_spectrum))
    joined = jnp.concatenate([masked_t.reshape(MM, NN, 2 * LEV), masked_p], axis=2)

    def legendre_slot(pair):
        values, coeffs = pair
        return jnp.dot(values, coeffs, preferred_element_type=jnp.float32).astype(jnp.bfloat16)

    four = lax.map(legendre_slot, (legendre, joined))
    four_t = four[:, :, :2 * LEV].reshape(MM, LAT, 2, LEV)
    four_p = four[:, :, 2 * LEV:]
    table = synth_table(m_order, NLON).reshape(MM * 2, NLON)
    rows = lax.broadcasted_iota(jnp.int32, (LEV, LEV), 0)
    cols = lax.broadcasted_iota(jnp.int32, (LEV, LEV), 1)
    hmat = jnp.where(cols >= rows, hydro_matrix, jnp.zeros_like(hydro_matrix)).astype(jnp.float32)

    def per_latitude(pair):
        coeff_t, coeff_p = pair
        temp_grid = jnp.dot(coeff_t.reshape(MM * 2, LEV).T, table, preferred_element_type=jnp.float32)
        surf_grid = jnp.dot(coeff_p.reshape(1, MM * 2), table, preferred_element_type=jnp.float32)[0]
        geopot = jnp.dot(hmat, temp_grid, precision=lax.Precision.HIGHEST) + surf_coupling[:, None] * surf_grid[None, :]
        return geopot.astype(jnp.bfloat16)

    geopot = lax.map(per_latitude, (jnp.moveaxis(four_t, 1, 0), jnp.moveaxis(four_p, 1, 0)))
    pool = jnp.transpose(geopot, (1, 0, 2)).reshape(LEV, LAT * NLON)
    slot_of = tap_index // BLK
    cell = tap_index % BLK
    block = jnp.take_along_axis(src_blocks, slot_of.reshape(NB, TAPS * BLK), axis=1).reshape(NB, TAPS, BLK)
    flat = block * BLK + cell

    def per_level(level_row):
        values = level_row[flat].astype(jnp.float32)
        return jnp.sum(values * tap_weight, axis=1)

    moved = lax.map(per_level, pool)
    return jnp.transpose(moved.reshape(LEV, LAT, NLON), (1, 0, 2))
```

```python
import functools
import math

import jax
import jax.numpy as jnp
from jax import lax
from jax.experimental import pallas as pl
from jax.experimental.pallas import tpu as pltpu
from jax.sharding import PartitionSpec as P

NLON = 5120
BLK = 128
TAPS = 4
XB = NLON // BLK
S = 20
CHUNKS = ((0, 8), (8, 8), (16, 4))
LOAD = 4
KP = 40
PR = 40
JJ = 6
HALF = 256
LATE = 58
MESH = pl.DeviceIdType.MESH
BF = jnp.bfloat16
F32 = jnp.float32


def iota(shape, dim):
    return lax.broadcasted_iota(jnp.int32, shape, dim)


def cosine(steps):
    steps = steps - NLON * jnp.floor(steps * (1.0 / NLON))
    y = (jnp.abs(steps * (1.0 / NLON) - 0.5) - 0.25) * (2.0 * math.pi)
    z = y * y
    p = -1.0 / 39916800.0
    for c in (1.0 / 362880.0, -1.0 / 5040.0, 1.0 / 120.0, -1.0 / 6.0, 1.0):
        p = p * z + c
    return y * p


def table_rows(m_ref, table, pair):
    row = iota((8, BLK), 0)
    point = iota((8, BLK), 1).astype(F32)
    first, second, turns = [], [], []
    for u in range(2):
        base = (pair * 2 + u) * S
        orders = []
        for start, count in CHUNKS:
            tile = jnp.zeros((8, BLK), F32)
            for i in range(8):
                value = m_ref[base + start + i % count].astype(F32)
                tile = jnp.where(row == i, value, tile)
            orders.append(tile)
        turn = [2.0 * cosine(o * float(BLK)) for o in orders]
        shift = jnp.where(row >= 4, NLON // 4, 0).astype(F32)
        for c, s in ((0, 0.0), (1, 0.0), (0, NLON / 4), (1, NLON / 4), (2, shift)):
            factor = jnp.where(orders[c] == 0.0, 1.0, 2.0)
            first.append(factor * cosine(orders[c] * point + s))
            second.append(factor * cosine(orders[c] * (point + float(BLK)) + s))
            turns.append(turn[c])
    old = jnp.concatenate(first, axis=0)
    new = jnp.concatenate(second, axis=0)
    turn = jnp.concatenate(turns, axis=0)
    place = pl.ds(pl.multiple_of(pair * 2 * PR, 16), 2 * PR)
    for x in range(XB):
        table[place, x * BLK : (x + 1) * BLK] = old.astype(BF)
        old, new = new, turn * new - old


def build_table(m_ref, table, nb):
    def pair(b, _):
        table_rows(m_ref, table, b)
        return 0

    lax.fori_loop(0, nb // 2, pair, 0)


def build_spread(idx, wgt, spread, first, last):
    cells = iota((HALF, BLK), 0).astype(BF)
    zero = jnp.zeros((HALF, BLK), BF)

    def block(b, _):
        index = idx[b]
        weight = wgt[b].astype(BF)
        for h in range(2):
            spot = (index - h * HALF).astype(F32).astype(BF)
            total = None
            for t in range(TAPS):
                hit = cells == jnp.broadcast_to(spot[t : t + 1, :], (HALF, BLK))
                part = jnp.where(hit, jnp.broadcast_to(weight[t : t + 1, :], (HALF, BLK)), zero)
                total = part if total is None else total + part
            spread[b, h * HALF : (h + 1) * HALF, :] = total
        return 0

    lax.fori_loop(first, last, block, 0)


def exchange_kernel(
    nb, nl, lat, lev_dev, early, *refs
):
    (temp_ref, surf_ref, leg_ref, ord_ref, h_ref, c_ref, idx_ref, wgt_ref), refs = refs[:8], refs[8:]
    out_ref, spread = refs[:2]
    table = refs[2] if early else None
    refs = refs[2 + early :]
    (buf, leg, h, coup, idx, wgt, m_ref, rows, gall, wide, total, pieces) = refs[:12]
    (sl, sm, sa, ra, sb, rb) = refs[12:]
    band = lax.axis_index("band")
    lev = lax.axis_index("lev")
    loads = S // LOAD

    def load_temp(d):
        part = pl.ds(d * LOAD, LOAD)
        return pltpu.make_async_copy(temp_ref.at[part], buf.at[part, pl.ds(0, lev_dev)], sl.at[d])

    def load_leg(d):
        part = pl.ds(d * LOAD, LOAD)
        return pltpu.make_async_copy(leg_ref.at[part], leg.at[part], sl.at[loads + d])

    load_surf = pltpu.make_async_copy(surf_ref, buf.at[:, lev_dev], sm.at[0])
    load_h = pltpu.make_async_copy(h_ref, h, sm.at[1])
    load_c = pltpu.make_async_copy(c_ref, coup, sm.at[2])
    load_idx = pltpu.make_async_copy(idx_ref, idx, sm.at[3])
    load_wgt = pltpu.make_async_copy(wgt_ref, wgt, sm.at[4])
    load_m = pltpu.make_async_copy(ord_ref, m_ref, sm.at[5])
    load_m.start()
    load_h.start()
    load_c.start()
    load_surf.start()
    for d in range(loads):
        load_leg(d).start()
        load_temp(d).start()
    load_idx.start()
    load_wgt.start()

    barrier = pltpu.get_barrier_semaphore()

    def greet_lev(i, _):
        pl.semaphore_signal(
            barrier, inc=1, device_id=(band, lax.rem(lev + i, nl)), device_id_type=MESH
        )
        return 0

    def greet_band(i, _):
        pl.semaphore_signal(
            barrier, inc=1, device_id=(lax.rem(band + i, nb), lev), device_id_type=MESH
        )
        return 0

    lax.fori_loop(1, nl, greet_lev, 0)
    lax.fori_loop(1, nb, greet_band, 0)

    depth = nl * BLK
    lev_total = h_ref.shape[1]
    load_h.wait()
    load_c.wait()
    row = iota((lev_dev, lev_total), 0) + lev * lev_dev
    col = iota((lev_dev, lev_total), 1)
    upper = jnp.where(col >= row, h[...].astype(F32), 0.0).astype(BF)
    row = iota((depth, lev_total), 0)
    col = iota((depth, lev_total), 1)
    spots = jnp.zeros((depth, lev_total), F32)
    for v in range(nl):
        place = row - v * BLK - 2 * (col - v * lev_dev)
        inside = (col >= v * lev_dev) & (col < (v + 1) * lev_dev)
        spots = jnp.where(inside & (place >= 0) & (place < 2), 1.0, spots)
    tall = lax.dot_general(
        spots.astype(BF), upper, (((1,), (1,)), ((), ())), preferred_element_type=F32
    )
    row = iota((depth, lev_dev), 0)
    high = coup[...].astype(BF).astype(F32)
    low = coup[...] - high
    mine = lev * BLK + 2 * lev_dev
    other = lax.rem(lev + 1, nl) * BLK + 2 * lev_dev
    tall = jnp.where(
        (row == mine) | (row == mine + 1), jnp.broadcast_to(high, (depth, lev_dev)), tall
    )
    tall = jnp.where(
        (row == other) | (row == other + 1), jnp.broadcast_to(low, (depth, lev_dev)), tall
    )
    tall = tall.astype(BF)
    row = iota((lev_dev, 2 * BLK), 0)
    col = iota((lev_dev, 2 * BLK), 1)
    odd = iota((depth, 2 * BLK), 0) & 1
    right = (iota((depth, 2 * BLK), 1) >= BLK).astype(jnp.int32)
    for t in range(3):
        place = jnp.where((col & (BLK - 1)) == row + t * KP, 1.0, 0.0).astype(BF)
        full = jnp.dot(tall, place, preferred_element_type=F32)
        wide[t] = jnp.where(odd == right, full, 0.0).astype(BF)

    def copy_a(i, c):
        start, count = CHUNKS[c]
        part = pl.ds(start * lat, count * lat)
        return pltpu.make_async_remote_copy(
            src_ref=gall.at[lev, part],
            dst_ref=gall.at[lev, part],
            send_sem=sa.at[c * nl + i],
            recv_sem=ra.at[c * nl + i],
            device_id=(band, lax.rem(lev + i, nl)),
            device_id_type=MESH,
        )

    width = leg_ref.shape[2]
    order = iota((lat, width), 1)
    blank = jnp.zeros((lat, BLK - 2 * lev_dev - 2), F32)
    load_m.wait()
    load_surf.wait()
    for c, (start, count) in enumerate(CHUNKS):
        for d in range(start // LOAD, (start + count) // LOAD):
            load_leg(d).wait()
            load_temp(d).wait()
            for u in range(LOAD):
                s = d * LOAD + u
                m = m_ref[band * S + s]
                keep = jnp.where(order >= m, 1.0, 0.0).astype(BF)
                values = leg[s] * keep
                coef = buf[s].reshape(2 * lev_dev + 2, width)
                four = lax.dot_general(
                    values, coef, (((1,), (1,)), ((), ())), preferred_element_type=F32
                )
                four = jnp.concatenate([four, blank], axis=1)
                rows[pl.ds(s - start, lat, stride=count), :] = four
        gall[lev, start * lat : (start + count) * lat, :] = rows[: count * lat, :].astype(BF)
        if c == 0:
            pl.semaphore_wait(barrier, nl - 1 + nb - 1)
        for i in range(1, nl):
            copy_a(i, c).start()

    load_idx.wait()
    load_wgt.wait()
    blocks = idx.shape[0]
    build_spread(idx, wgt, spread, 0, blocks - LATE)

    for c in range(len(CHUNKS)):
        for i in range(1, nl):
            copy_a(i, c).wait()

    group = 16
    total[...] = jnp.zeros_like(total)

    def hydro(g, _):
        parts = []
        for start, count in CHUNKS:
            size = count * group
            parts.append((pl.ds(pl.multiple_of(start * lat + g * size, 16), size), size))
        left = jnp.concatenate(
            [jnp.concatenate([gall[v, p] for v in range(nl)], axis=1) for p, _ in parts], axis=0
        )
        for t in range(3):
            full = jnp.dot(left, wide[t], preferred_element_type=F32)
            for p in range(group // 2):
                at = 0
                mine = []
                for start, count in CHUNKS:
                    mine.append(full[at + p * 2 * count : at + (p + 1) * 2 * count])
                    at += count * group
                place = g * (group // 2) + p + 2 - t
                total[place] = total[place] + jnp.concatenate(mine, axis=0)
        return 0

    lax.fori_loop(0, lat // group, hydro, 0)

    def pack(b, _):
        value = total[b + 1]
        value = jnp.concatenate([value[:, :BLK], value[:, BLK:]], axis=0)
        pieces[b] = value.astype(BF)
        return 0

    lax.fori_loop(0, nb, pack, 0)

    def copy_b(i):
        peer = lax.rem(band + i, nb)
        return pltpu.make_async_remote_copy(
            src_ref=pieces.at[peer],
            dst_ref=out_ref.at[band],
            send_sem=sb.at[i],
            recv_sem=rb.at[i],
            device_id=(peer, lev),
            device_id_type=MESH,
        )

    def send(i, _):
        copy_b(i).start()
        return 0

    lax.fori_loop(1, nb, send, 0)
    out_ref[band] = pieces[band]
    build_spread(idx, wgt, spread, blocks - LATE, blocks)
    if early:
        build_table(m_ref, table, nb)

    def done(i, _):
        copy_b(i).wait()
        return 0

    lax.fori_loop(1, nb, done, 0)


def exchange(temp, surf, legendre, m_order, hydro, coupling, idx, wgt, nb, nl, early):
    _, lev_dev, _, width = temp.shape
    lat = legendre.shape[1]
    blocks = idx.shape[0]
    vmem = pl.BlockSpec(memory_space=pltpu.VMEM)
    hbm = pl.BlockSpec(memory_space=pltpu.HBM)
    out_shape = [
        jax.ShapeDtypeStruct((nb, 2 * PR, BLK), BF),
        jax.ShapeDtypeStruct((blocks, 2 * HALF, BLK), BF),
    ]
    if early:
        out_shape.append(jax.ShapeDtypeStruct((nb * PR, NLON), BF))
    return pl.pallas_call(
        functools.partial(exchange_kernel, nb, nl, lat, lev_dev, early),
        out_shape=out_shape,
        in_specs=[hbm] * 8,
        out_specs=[vmem] * len(out_shape),
        scratch_shapes=[
            pltpu.VMEM((S, lev_dev + 1, 2, width), BF),
            pltpu.VMEM(legendre.shape, BF),
            pltpu.VMEM(hydro.shape, BF),
            pltpu.VMEM(coupling.shape, F32),
            pltpu.VMEM(idx.shape, jnp.int32),
            pltpu.VMEM(wgt.shape, F32),
            pltpu.SMEM(m_order.shape, jnp.int32),
            pltpu.VMEM((8 * lat, BLK), F32),
            pltpu.VMEM((nl, S * lat, BLK), BF),
            pltpu.VMEM((3, nl * BLK, 2 * BLK), BF),
            pltpu.VMEM((nb + 2, PR, 2 * BLK), F32),
            pltpu.VMEM((nb, 2 * PR, BLK), BF),
            pltpu.SemaphoreType.DMA((2 * (S // LOAD),)),
            pltpu.SemaphoreType.DMA((6,)),
            pltpu.SemaphoreType.DMA((len(CHUNKS) * nl,)),
            pltpu.SemaphoreType.DMA((len(CHUNKS) * nl,)),
            pltpu.SemaphoreType.DMA((nb,)),
            pltpu.SemaphoreType.DMA((nb,)),
        ],
        compiler_params=pltpu.CompilerParams(
            collective_id=0, has_side_effects=True, vmem_limit_bytes=(30 if early else 52) * 1024 * 1024
        ),
    )(*[
        pltpu.with_memory_space_constraint(x, pltpu.HBM)
        for x in (temp, surf, legendre, m_order, hydro, coupling, idx, wgt)
    ])


def grid_kernel(nb, lev_dev, early, src_ref, m_ref, coef_ref, spread, *refs):
    if early:
        table, out_ref, pool = refs
    else:
        out_ref, pool, table = refs
        build_table(m_ref, table, nb)
    coef = coef_ref[...].astype(F32)
    left = []
    for p in range(2):
        tiles = []
        for b in range(nb):
            value = coef[b]
            for r in range(2):
                for c in range(2):
                    at = r * PR + c * 16 + p * 8
                    tiles.append(value[at : at + 8])
            for r in range(2):
                at = r * PR + 32 + p * 4
                tiles.append(value[at : at + 4])
        left.append(jnp.concatenate(tiles, axis=0).T)
    left = jnp.concatenate(left, axis=0).astype(BF)
    group = 4

    def synth(c, _):
        cols = pl.ds(pl.multiple_of(c * (group * BLK), 128), group * BLK)
        grid = jnp.dot(left, table[:, cols], preferred_element_type=F32).astype(BF)
        for t in range(3):
            for p in range(2):
                at = p * BLK + t * KP
                for g in range(group):
                    pool[(2 * t + p) * XB + c * group + g] = grid[
                        at : at + KP, g * BLK : (g + 1) * BLK
                    ]
        return 0

    lax.fori_loop(0, XB // group, synth, 0)

    first = (lax.axis_index("band") - 1) * (2 * XB)

    def read(b):
        source = jnp.concatenate([pool[src_ref[i, b] - first] for i in range(4)], axis=1)
        return jnp.dot(source, spread[b], preferred_element_type=F32)

    for j in range(2):

        def step(x, _):
            for u in range(8):
                xb = x * 8 + u
                out_ref[:, j, pl.ds(pl.multiple_of(xb * BLK, 128), BLK)] = read(j * XB + xb)[
                    :lev_dev
                ]
            return 0

        lax.fori_loop(0, XB // 8, step, 0)


def grid_part(src, m_order, coef, spread, table, nb, lev_dev):
    vmem = pl.BlockSpec(memory_space=pltpu.VMEM)
    smem = pl.BlockSpec(memory_space=pltpu.SMEM)
    early = len(table) > 0
    scratch = [pltpu.VMEM((JJ * XB, KP, BLK), BF)]
    if not early:
        scratch.append(pltpu.VMEM((nb * PR, NLON), BF))
    return pl.pallas_call(
        functools.partial(grid_kernel, nb, lev_dev, early),
        out_shape=jax.ShapeDtypeStruct((lev_dev, 2, NLON), F32),
        in_specs=[smem, smem] + [vmem] * (2 + len(table)),
        out_specs=vmem,
        scratch_shapes=scratch,
        compiler_params=pltpu.CompilerParams(
            vmem_limit_bytes=(24 if early else 52) * 1024 * 1024
        ),
    )(src, m_order, coef, spread, *table)


def shards(
    temp_spectrum,
    surf_spectrum,
    legendre,
    m_order,
    hydro_matrix,
    surf_coupling,
    src_blocks,
    tap_index,
    tap_weight,
):
    lev_dev = temp_spectrum.shape[3]
    nb, nl = lax.axis_size("band"), lax.axis_size("lev")
    early = nb <= 16
    coef, spread, *table = exchange(
        jnp.transpose(temp_spectrum, (0, 3, 2, 1)),
        jnp.transpose(surf_spectrum, (0, 2, 1)),
        legendre,
        m_order,
        hydro_matrix,
        surf_coupling[None, :],
        tap_index,
        tap_weight,
        nb,
        nl,
        early,
    )
    out = grid_part(src_blocks.T, m_order, coef, spread, table, nb, lev_dev)
    return jnp.transpose(out, (1, 0, 2))


def solution(mesh):
    in_specs = (
        P("band", None, None, "lev"),
        P("band", None, None),
        P("band", None, None),
        P(),
        P("lev", None),
        P("lev"),
        P("band", None),
        P("band", None, None),
        P("band", None, None),
    )
    out_specs = P("band", "lev", None)
    return jax.shard_map(shards, mesh=mesh, in_specs=in_specs, out_specs=out_specs, check_vma=False)
```

```python
import functools
import math

import jax
import jax.numpy as jnp
from jax import lax
from jax.experimental import pallas as pl
from jax.experimental.pallas import tpu as pltpu
from jax.sharding import PartitionSpec as P

NLON = 5120
BLK = 128
TAPS = 4
XB = NLON // BLK
S = 20
CHUNKS = ((0, 8), (8, 8), (16, 4))
KP = 40
PR = 40
JJ = 6
HALF = 256
LATE = 46
STEP = 5
MESH = pl.DeviceIdType.MESH
BF = jnp.bfloat16
F32 = jnp.float32


def iota(shape, dim):
    return lax.broadcasted_iota(jnp.int32, shape, dim)


def cosine(steps):
    steps = steps - NLON * jnp.floor(steps * (1.0 / NLON))
    y = (jnp.abs(steps * (1.0 / NLON) - 0.5) - 0.25) * (2.0 * math.pi)
    z = y * y
    p = -1.0 / 39916800.0
    for c in (1.0 / 362880.0, -1.0 / 5040.0, 1.0 / 120.0, -1.0 / 6.0, 1.0):
        p = p * z + c
    return y * p


def table_rows(m_ref, table, pair):
    row = iota((8, BLK), 0)
    point = iota((8, BLK), 1).astype(F32)
    first, second, turns = [], [], []
    for u in range(2):
        base = (pair * 2 + u) * S
        orders = []
        for start, count in CHUNKS:
            tile = jnp.zeros((8, BLK), F32)
            for i in range(8):
                value = m_ref[base + start + i % count].astype(F32)
                tile = jnp.where(row == i, value, tile)
            orders.append(tile)
        turn = [2.0 * cosine(o * float(BLK)) for o in orders]
        shift = jnp.where(row >= 4, NLON // 4, 0).astype(F32)
        for c, s in ((0, 0.0), (1, 0.0), (0, NLON / 4), (1, NLON / 4), (2, shift)):
            factor = jnp.where(orders[c] == 0.0, 1.0, 2.0)
            first.append(factor * cosine(orders[c] * point + s))
            second.append(factor * cosine(orders[c] * (point + float(BLK)) + s))
            turns.append(turn[c])
    old = jnp.concatenate(first, axis=0)
    new = jnp.concatenate(second, axis=0)
    turn = jnp.concatenate(turns, axis=0)
    place = pl.ds(pl.multiple_of(pair * 2 * PR, 16), 2 * PR)
    for x in range(XB):
        table[place, x * BLK : (x + 1) * BLK] = old.astype(BF)
        old, new = new, turn * new - old


def build_table(m_ref, table, nb):
    def pair(b, _):
        table_rows(m_ref, table, b)
        return 0

    lax.fori_loop(0, nb // 2, pair, 0)


def build_spread(idx, wgt, spread, first, last):
    cells = iota((HALF, BLK), 0).astype(BF)
    zero = jnp.zeros((HALF, BLK), BF)

    def block(b, _):
        index = idx[b]
        weight = wgt[b].astype(BF)
        for h in range(2):
            spot = (index - h * HALF).astype(F32).astype(BF)
            total = None
            for t in range(TAPS):
                hit = cells == jnp.broadcast_to(spot[t : t + 1, :], (HALF, BLK))
                part = jnp.where(hit, jnp.broadcast_to(weight[t : t + 1, :], (HALF, BLK)), zero)
                total = part if total is None else total + part
            spread[b, h * HALF : (h + 1) * HALF, :] = total
        return 0

    lax.fori_loop(first, last, block, 0)


def exchange_kernel(
    nb, nl, lat, lev_dev, early, *refs
):
    (temp_ref, surf_ref, leg_ref, ord_ref, h_ref, c_ref, idx_ref, wgt_ref), refs = refs[:8], refs[8:]
    out_ref, spread = refs[:2]
    table = refs[2] if early else None
    refs = refs[2 + early :]
    (buf, leg, h, coup, idx, wgt, m_ref, rows, gall, wide, total, pieces) = refs[:12]
    (sl, sm, sa, ra, sb, rb) = refs[12:]
    band = lax.axis_index("band")
    lev = lax.axis_index("lev")
    chunks = len(CHUNKS)

    def load_temp(c):
        part = pl.ds(*CHUNKS[c])
        return pltpu.make_async_copy(temp_ref.at[part], buf.at[part, pl.ds(0, lev_dev)], sl.at[c])

    def load_leg(c):
        part = pl.ds(*CHUNKS[c])
        return pltpu.make_async_copy(leg_ref.at[part], leg.at[part], sl.at[chunks + c])

    load_surf = pltpu.make_async_copy(surf_ref, buf.at[:, lev_dev], sm.at[0])
    load_h = pltpu.make_async_copy(h_ref, h, sm.at[1])
    load_c = pltpu.make_async_copy(c_ref, coup, sm.at[2])
    load_idx = pltpu.make_async_copy(idx_ref, idx, sm.at[3])
    load_wgt = pltpu.make_async_copy(wgt_ref, wgt, sm.at[4])
    load_m = pltpu.make_async_copy(ord_ref, m_ref, sm.at[5])
    load_m.start()
    load_surf.start()
    load_leg(0).start()
    load_temp(0).start()

    barrier = pltpu.get_barrier_semaphore()

    def greet_lev(i, _):
        pl.semaphore_signal(
            barrier, inc=1, device_id=(band, lax.rem(lev + i, nl)), device_id_type=MESH
        )
        return 0

    def greet_band(i, _):
        pl.semaphore_signal(
            barrier, inc=1, device_id=(lax.rem(band + i, nb), lev), device_id_type=MESH
        )
        return 0

    lax.fori_loop(1, nb, greet_band, 0)
    lax.fori_loop(1, nl, greet_lev, 0)
    for c in range(1, chunks):
        load_leg(c).start()
        load_temp(c).start()
    load_h.start()
    load_c.start()
    load_idx.start()
    load_wgt.start()

    def copy_a(i, c):
        start, count = CHUNKS[c]
        part = pl.ds(start * lat, count * lat)
        return pltpu.make_async_remote_copy(
            src_ref=gall.at[lev, part],
            dst_ref=gall.at[lev, part],
            send_sem=sa.at[c * nl + i],
            recv_sem=ra.at[c * nl + i],
            device_id=(band, lax.rem(lev + i, nl)),
            device_id_type=MESH,
        )

    width = leg_ref.shape[2]
    order = iota((lat, width), 1)
    blank = jnp.zeros((lat, BLK - 2 * lev_dev - 2), F32)
    load_m.wait()
    load_surf.wait()
    for c, (start, count) in enumerate(CHUNKS):
        load_leg(c).wait()
        load_temp(c).wait()
        for s in range(start, start + count):
            m = m_ref[band * S + s]
            keep = jnp.where(order >= m, 1.0, 0.0).astype(BF)
            values = leg[s] * keep
            coef = buf[s].reshape(2 * lev_dev + 2, width)
            four = lax.dot_general(
                values, coef, (((1,), (1,)), ((), ())), preferred_element_type=F32
            )
            four = jnp.concatenate([four, blank], axis=1)
            rows[pl.ds(s - start, lat, stride=count), :] = four
        gall[lev, start * lat : (start + count) * lat, :] = rows[: count * lat, :].astype(BF)
        if c == 1:
            pl.semaphore_wait(barrier, nl - 1 + nb - 1)
        if c >= 1:
            for d in range(c - 1 if c == 1 else c, c + 1):
                for i in range(1, nl):
                    copy_a(i, d).start()

    depth = nl * BLK
    lev_total = h_ref.shape[1]
    load_h.wait()
    load_c.wait()
    row = iota((lev_dev, lev_total), 0) + lev * lev_dev
    col = iota((lev_dev, lev_total), 1)
    upper = jnp.where(col >= row, h[...].astype(F32), 0.0).astype(BF)
    row = iota((depth, lev_total), 0)
    col = iota((depth, lev_total), 1)
    spots = jnp.zeros((depth, lev_total), F32)
    for v in range(nl):
        place = row - v * BLK - 2 * (col - v * lev_dev)
        inside = (col >= v * lev_dev) & (col < (v + 1) * lev_dev)
        spots = jnp.where(inside & (place >= 0) & (place < 2), 1.0, spots)
    tall = lax.dot_general(
        spots.astype(BF), upper, (((1,), (1,)), ((), ())), preferred_element_type=F32
    )
    row = iota((depth, lev_dev), 0)
    high = coup[...].astype(BF).astype(F32)
    low = coup[...] - high
    mine = lev * BLK + 2 * lev_dev
    other = lax.rem(lev + 1, nl) * BLK + 2 * lev_dev
    tall = jnp.where(
        (row == mine) | (row == mine + 1), jnp.broadcast_to(high, (depth, lev_dev)), tall
    )
    tall = jnp.where(
        (row == other) | (row == other + 1), jnp.broadcast_to(low, (depth, lev_dev)), tall
    )
    tall = tall.astype(BF)
    row = iota((lev_dev, 2 * BLK), 0)
    col = iota((lev_dev, 2 * BLK), 1)
    odd = iota((depth, 2 * BLK), 0) & 1
    right = (iota((depth, 2 * BLK), 1) >= BLK).astype(jnp.int32)
    for t in range(3):
        place = jnp.where((col & (BLK - 1)) == row + t * KP, 1.0, 0.0).astype(BF)
        full = jnp.dot(tall, place, preferred_element_type=F32)
        wide[t] = jnp.where(odd == right, full, 0.0).astype(BF)

    load_idx.wait()
    load_wgt.wait()
    blocks = idx.shape[0]
    build_spread(idx, wgt, spread, 0, blocks - LATE)

    for c in range(len(CHUNKS)):
        for i in range(1, nl):
            copy_a(i, c).wait()

    group = 16
    pairs = group // 2

    def hydro(g):
        parts = []
        for start, count in CHUNKS:
            size = count * group
            at = start * lat + g * size
            parts.append((pl.ds(at if isinstance(at, int) else pl.multiple_of(at, 16), size), size))
        left = jnp.concatenate(
            [jnp.concatenate([gall[v, p] for v in range(nl)], axis=1) for p, _ in parts], axis=0
        )
        result = []
        for t in range(3):
            full = jnp.dot(left, wide[t], preferred_element_type=F32)
            split = []
            for p in range(pairs):
                at = 0
                mine = []
                for start, count in CHUNKS:
                    mine.append(full[at + p * 2 * count : at + (p + 1) * 2 * count])
                    at += count * group
                split.append(jnp.concatenate(mine, axis=0))
            result.append(split)
        return result

    def pack(b, value):
        value = jnp.concatenate([value[:, :BLK], value[:, BLK:]], axis=0)
        pieces[b] = value.astype(BF)

    if lat == group:
        result = hydro(0)
        for b in range(nb):
            value = result[1][b]
            for t in (0, 2):
                if 0 <= b - 1 + t < pairs:
                    value = value + result[t][b - 1 + t]
            pack(b, value)
    else:
        total[...] = jnp.zeros_like(total)

        def many(g, _):
            result = hydro(g)
            for t in range(3):
                for p in range(pairs):
                    place = g * pairs + p + 2 - t
                    total[place] = total[place] + result[t][p]
            return 0

        def finish(b, _):
            pack(b, total[b + 1])
            return 0

        lax.fori_loop(0, lat // group, many, 0)
        lax.fori_loop(0, nb, finish, 0)

    def copy_b(i):
        peer = lax.rem(band + i, nb)
        return pltpu.make_async_remote_copy(
            src_ref=pieces.at[peer],
            dst_ref=out_ref.at[band],
            send_sem=sb.at[i],
            recv_sem=rb.at[i],
            device_id=(peer, lev),
            device_id_type=MESH,
        )

    def send(i, _):
        copy_b(i).start()
        return 0

    lax.fori_loop(1, nb, send, 0)
    out_ref[band] = pieces[band]
    build_spread(idx, wgt, spread, blocks - LATE, blocks)
    if early:
        build_table(m_ref, table, nb)

    def done(i, _):
        copy_b(i).wait()
        return 0

    lax.fori_loop(1, nb, done, 0)


def exchange(temp, surf, legendre, m_order, hydro, coupling, idx, wgt, nb, nl, early):
    _, lev_dev, _, width = temp.shape
    lat = legendre.shape[1]
    blocks = idx.shape[0]
    vmem = pl.BlockSpec(memory_space=pltpu.VMEM)
    hbm = pl.BlockSpec(memory_space=pltpu.HBM)
    out_shape = [
        jax.ShapeDtypeStruct((nb, 2 * PR, BLK), BF),
        jax.ShapeDtypeStruct((blocks, 2 * HALF, BLK), BF),
    ]
    if early:
        out_shape.append(jax.ShapeDtypeStruct((nb * PR, NLON), BF))
    return pl.pallas_call(
        functools.partial(exchange_kernel, nb, nl, lat, lev_dev, early),
        out_shape=out_shape,
        in_specs=[hbm] * 8,
        out_specs=[vmem] * len(out_shape),
        scratch_shapes=[
            pltpu.VMEM((S, lev_dev + 1, 2, width), BF),
            pltpu.VMEM(legendre.shape, BF),
            pltpu.VMEM(hydro.shape, BF),
            pltpu.VMEM(coupling.shape, F32),
            pltpu.VMEM(idx.shape, jnp.int32),
            pltpu.VMEM(wgt.shape, F32),
            pltpu.SMEM(m_order.shape, jnp.int32),
            pltpu.VMEM((8 * lat, BLK), F32),
            pltpu.VMEM((nl, S * lat, BLK), BF),
            pltpu.VMEM((3, nl * BLK, 2 * BLK), BF),
            pltpu.VMEM((nb + 2 if lat > 16 else 1, PR, 2 * BLK), F32),
            pltpu.VMEM((nb, 2 * PR, BLK), BF),
            pltpu.SemaphoreType.DMA((2 * len(CHUNKS),)),
            pltpu.SemaphoreType.DMA((6,)),
            pltpu.SemaphoreType.DMA((len(CHUNKS) * nl,)),
            pltpu.SemaphoreType.DMA((len(CHUNKS) * nl,)),
            pltpu.SemaphoreType.DMA((nb,)),
            pltpu.SemaphoreType.DMA((nb,)),
        ],
        compiler_params=pltpu.CompilerParams(
            collective_id=0, has_side_effects=True, vmem_limit_bytes=(30 if early else 52) * 1024 * 1024
        ),
    )(*[
        pltpu.with_memory_space_constraint(x, pltpu.HBM)
        for x in (temp, surf, legendre, m_order, hydro, coupling, idx, wgt)
    ])


def grid_kernel(nb, lev_dev, early, src_ref, coef_ref, spread, *refs):
    if early:
        table, out_ref, src, pool, grid, ss, so = refs
    else:
        m_ref, out_ref, src, pool, grid, ss, so, table = refs
        build_table(m_ref, table, nb)
    load_src = pltpu.make_async_copy(src_ref, src, ss)
    load_src.start()
    coef = coef_ref[...].astype(F32)
    left = []
    for p in range(2):
        tiles = []
        for b in range(nb):
            value = coef[b]
            for r in range(2):
                for c in range(2):
                    at = r * PR + c * 16 + p * 8
                    tiles.append(value[at : at + 8])
            for r in range(2):
                at = r * PR + 32 + p * 4
                tiles.append(value[at : at + 4])
        left.append(jnp.concatenate(tiles, axis=0).T)
    left = jnp.concatenate(left, axis=0).astype(BF)
    group = 4

    def synth(c, _):
        cols = pl.ds(pl.multiple_of(c * (group * BLK), 128), group * BLK)
        value = jnp.dot(left, table[:, cols], preferred_element_type=F32).astype(BF)
        for t in range(3):
            for p in range(2):
                at = p * BLK + t * KP
                for g in range(group):
                    pool[(2 * t + p) * XB + c * group + g] = value[
                        at : at + KP, g * BLK : (g + 1) * BLK
                    ]
        return 0

    lax.fori_loop(0, XB // group, synth, 0, unroll=XB // group if early else 1)
    load_src.wait()

    first = (lax.axis_index("band") - 1) * (2 * XB)

    def read(b):
        source = jnp.concatenate([pool[src[i, b] - first] for i in range(4)], axis=1)
        return jnp.dot(source, spread[b], preferred_element_type=F32)

    def write(q):
        cols = pl.ds(q * (STEP * BLK), STEP * BLK)
        return pltpu.make_async_copy(grid.at[:, :, cols], out_ref.at[:, :, cols], so.at[q])

    for q in range(XB // STEP):
        for x in range(q * STEP, (q + 1) * STEP):
            for j in range(2):
                grid[:, j, x * BLK : (x + 1) * BLK] = read(j * XB + x)[:lev_dev]
        write(q).start()
    for q in range(XB // STEP):
        write(q).wait()


def grid_part(src, m_order, coef, spread, table, nb, lev_dev):
    vmem = pl.BlockSpec(memory_space=pltpu.VMEM)
    hbm = pl.BlockSpec(memory_space=pltpu.HBM)
    early = len(table) > 0
    scratch = [
        pltpu.SMEM(src.shape, jnp.int32),
        pltpu.VMEM((JJ * XB, KP, BLK), BF),
        pltpu.VMEM((lev_dev, 2, NLON), F32),
        pltpu.SemaphoreType.DMA,
        pltpu.SemaphoreType.DMA((XB // STEP,)),
    ]
    src = pltpu.with_memory_space_constraint(src, pltpu.HBM)
    if early:
        last, specs = list(table), [vmem]
    else:
        last, specs = [m_order], [pl.BlockSpec(memory_space=pltpu.SMEM)]
        scratch.append(pltpu.VMEM((nb * PR, NLON), BF))
    return pl.pallas_call(
        functools.partial(grid_kernel, nb, lev_dev, early),
        out_shape=jax.ShapeDtypeStruct((lev_dev, 2, NLON), F32),
        in_specs=[hbm, vmem, vmem] + specs,
        out_specs=hbm,
        scratch_shapes=scratch,
        compiler_params=pltpu.CompilerParams(
            vmem_limit_bytes=(24 if early else 54) * 1024 * 1024
        ),
    )(src, coef, spread, *last)


def shards(
    temp_spectrum,
    surf_spectrum,
    legendre,
    m_order,
    hydro_matrix,
    surf_coupling,
    src_blocks,
    tap_index,
    tap_weight,
):
    lev_dev = temp_spectrum.shape[3]
    nb, nl = lax.axis_size("band"), lax.axis_size("lev")
    early = nb <= 16
    coef, spread, *table = exchange(
        jnp.transpose(temp_spectrum, (0, 3, 2, 1)),
        jnp.transpose(surf_spectrum, (0, 2, 1)),
        legendre,
        m_order,
        hydro_matrix,
        surf_coupling[None, :],
        tap_index,
        tap_weight,
        nb,
        nl,
        early,
    )
    out = grid_part(src_blocks.T, m_order, coef, spread, table, nb, lev_dev)
    return jnp.transpose(out, (1, 0, 2))


def solution(mesh):
    in_specs = (
        P("band", None, None, "lev"),
        P("band", None, None),
        P("band", None, None),
        P(),
        P("lev", None),
        P("lev"),
        P("band", None),
        P("band", None, None),
        P("band", None, None),
    )
    out_specs = P("band", "lev", None)
    return jax.shard_map(shards, mesh=mesh, in_specs=in_specs, out_specs=out_specs, check_vma=False)
```

```python
import functools
import math

import jax
import jax.numpy as jnp
from jax import lax
from jax.experimental import pallas as pl
from jax.experimental.pallas import tpu as pltpu
from jax.sharding import PartitionSpec as P

NLON = 5120
BLK = 128
TAPS = 4
XB = NLON // BLK
S = 20
CHUNKS = ((0, 8), (8, 8), (16, 4))
Q = 4
BLOCKS = S // Q
KP = 40
PR = 40
JJ = 6
HALF = 256
LATE = 46
STEP = 5
MESH = pl.DeviceIdType.MESH
BF = jnp.bfloat16
F32 = jnp.float32


def iota(shape, dim):
    return lax.broadcasted_iota(jnp.int32, shape, dim)


def cosine(steps):
    steps = steps - NLON * jnp.floor(steps * (1.0 / NLON))
    y = (jnp.abs(steps * (1.0 / NLON) - 0.5) - 0.25) * (2.0 * math.pi)
    z = y * y
    p = -1.0 / 39916800.0
    for c in (1.0 / 362880.0, -1.0 / 5040.0, 1.0 / 120.0, -1.0 / 6.0, 1.0):
        p = p * z + c
    return y * p


def table_rows(m_ref, table, pair):
    row = iota((8, BLK), 0)
    point = iota((8, BLK), 1).astype(F32)
    first, second, turns = [], [], []
    for u in range(2):
        base = (pair * 2 + u) * S
        orders = []
        for start, count in CHUNKS:
            tile = jnp.zeros((8, BLK), F32)
            for i in range(8):
                value = m_ref[base + start + i % count].astype(F32)
                tile = jnp.where(row == i, value, tile)
            orders.append(tile)
        turn = [2.0 * cosine(o * float(BLK)) for o in orders]
        shift = jnp.where(row >= 4, NLON // 4, 0).astype(F32)
        for c, s in ((0, 0.0), (1, 0.0), (0, NLON / 4), (1, NLON / 4), (2, shift)):
            factor = jnp.where(orders[c] == 0.0, 1.0, 2.0)
            first.append(factor * cosine(orders[c] * point + s))
            second.append(factor * cosine(orders[c] * (point + float(BLK)) + s))
            turns.append(turn[c])
    old = jnp.concatenate(first, axis=0)
    new = jnp.concatenate(second, axis=0)
    turn = jnp.concatenate(turns, axis=0)
    place = pl.ds(pl.multiple_of(pair * 2 * PR, 16), 2 * PR)
    for x in range(XB):
        table[place, x * BLK : (x + 1) * BLK] = old.astype(BF)
        old, new = new, turn * new - old


def build_table(m_ref, table, nb):
    def pair(b, _):
        table_rows(m_ref, table, b)
        return 0

    lax.fori_loop(0, nb // 2, pair, 0)


def build_spread(idx, wgt, spread, first, last):
    cells = iota((HALF, BLK), 0).astype(BF)
    zero = jnp.zeros((HALF, BLK), BF)

    def block(b, _):
        index = idx[b]
        weight = wgt[b].astype(BF)
        for h in range(2):
            spot = (index - h * HALF).astype(F32).astype(BF)
            total = None
            for t in range(TAPS):
                hit = cells == jnp.broadcast_to(spot[t : t + 1, :], (HALF, BLK))
                part = jnp.where(hit, jnp.broadcast_to(weight[t : t + 1, :], (HALF, BLK)), zero)
                total = part if total is None else total + part
            spread[b, h * HALF : (h + 1) * HALF, :] = total
        return 0

    lax.fori_loop(first, last, block, 0)


def exchange_kernel(
    nb, nl, lat, lev_dev, early, *refs
):
    (temp_ref, surf_ref, leg_ref, ord_ref, h_ref, c_ref, idx_ref, wgt_ref), refs = refs[:8], refs[8:]
    out_ref, spread = refs[:2]
    table = refs[2] if early else None
    refs = refs[2 + early :]
    (buf, leg, h, coup, idx, wgt, m_ref, rows, gall, full, wide, total, pieces) = refs[:13]
    (sl, sm, sa, ra, sb, rb) = refs[13:]
    band = lax.axis_index("band")
    lev = lax.axis_index("lev")
    chunks = len(CHUNKS)

    def load_temp(c):
        part = pl.ds(*CHUNKS[c])
        return pltpu.make_async_copy(temp_ref.at[part], buf.at[part, pl.ds(0, lev_dev)], sl.at[c])

    def load_leg(c):
        part = pl.ds(*CHUNKS[c])
        return pltpu.make_async_copy(leg_ref.at[part], leg.at[part], sl.at[chunks + c])

    load_surf = pltpu.make_async_copy(surf_ref, buf.at[:, lev_dev], sm.at[0])
    load_h = pltpu.make_async_copy(h_ref, h, sm.at[1])
    load_c = pltpu.make_async_copy(c_ref, coup, sm.at[2])
    load_idx = pltpu.make_async_copy(idx_ref, idx, sm.at[3])
    load_wgt = pltpu.make_async_copy(wgt_ref, wgt, sm.at[4])
    load_m = pltpu.make_async_copy(ord_ref, m_ref, sm.at[5])
    load_m.start()
    load_surf.start()
    load_leg(0).start()
    load_temp(0).start()

    barrier = pltpu.get_barrier_semaphore()

    def greet_lev(i, _):
        pl.semaphore_signal(
            barrier, inc=1, device_id=(band, lax.rem(lev + i, nl)), device_id_type=MESH
        )
        return 0

    def greet_band(i, _):
        pl.semaphore_signal(
            barrier, inc=1, device_id=(lax.rem(band + i, nb), lev), device_id_type=MESH
        )
        return 0

    lax.fori_loop(1, nb, greet_band, 0)
    lax.fori_loop(1, nl, greet_lev, 0)
    for c in range(1, chunks):
        load_leg(c).start()
        load_temp(c).start()
    load_h.start()
    load_c.start()
    load_idx.start()
    load_wgt.start()

    def copy_a(i, c):
        part = pl.ds(c * Q * lat, Q * lat)
        return pltpu.make_async_remote_copy(
            src_ref=gall.at[lev, part],
            dst_ref=gall.at[lev, part],
            send_sem=sa.at[c * nl + i],
            recv_sem=ra.at[c * nl + i],
            device_id=(band, lax.rem(lev + i, nl)),
            device_id_type=MESH,
        )

    width = leg_ref.shape[2]
    used = 2 * lev_dev
    tail = 2 * used - BLK
    spare = used + 4
    order = iota((lat, width), 1)
    lane = iota((lat, BLK), 1)
    blank = jnp.zeros((lat, BLK - used - 2), F32)

    def transform(s):
        m = m_ref[band * S + s]
        keep = jnp.where(order >= m, 1.0, 0.0).astype(BF)
        coef = buf[s].reshape(used + 2, width)
        four = lax.dot_general(
            leg[s] * keep, coef, (((1,), (1,)), ((), ())), preferred_element_type=F32
        )
        return jnp.concatenate([four, blank], axis=1)

    def place(block, q, value):
        rows[block, pl.ds(q, lat, stride=Q), :] = value

    load_m.wait()
    load_surf.wait()
    ends = [None] * Q
    for c, (start, count) in enumerate(CHUNKS):
        load_leg(c).wait()
        load_temp(c).wait()
        for q in range(Q):
            one = transform(start + q)
            place(start // Q, q, one)
            if count == 2 * Q:
                two = transform(start + Q + q)
                place(start // Q + 1, q, two)
                place(BLOCKS + c, q, jnp.where(lane < used, one, pltpu.roll(two, used, 1)))
                end = pltpu.roll(two, spare + c * tail - used + tail, 1)
                ends[q] = end if c == 0 else jnp.where(lane < spare + c * tail, ends[q], end)
            else:
                place(BLOCKS + c, q, jnp.where(lane < used, one, ends[q]))
        gall[lev, c * Q * lat : (c + 1) * Q * lat, :] = rows[BLOCKS + c].astype(BF)
        if c == 1:
            pl.semaphore_wait(barrier, nl - 1 + nb - 1)
        if c >= 1:
            for d in range(c - 1 if c == 1 else c, c + 1):
                for i in range(1, nl):
                    copy_a(i, d).start()
    for k in range(BLOCKS):
        full[lev, k * Q * lat : (k + 1) * Q * lat, :] = rows[k].astype(BF)

    depth = nl * BLK
    lev_total = h_ref.shape[1]
    load_h.wait()
    load_c.wait()
    row = iota((lev_dev, lev_total), 0) + lev * lev_dev
    col = iota((lev_dev, lev_total), 1)
    upper = jnp.where(col >= row, h[...].astype(F32), 0.0).astype(BF)
    row = iota((depth, lev_total), 0)
    col = iota((depth, lev_total), 1)
    spots = jnp.zeros((depth, lev_total), F32)
    for v in range(nl):
        step = row - v * BLK - 2 * (col - v * lev_dev)
        inside = (col >= v * lev_dev) & (col < (v + 1) * lev_dev)
        spots = jnp.where(inside & (step >= 0) & (step < 2), 1.0, spots)
    tall = lax.dot_general(
        spots.astype(BF), upper, (((1,), (1,)), ((), ())), preferred_element_type=F32
    )
    row = iota((depth, lev_dev), 0)
    mine = lev * BLK + 2 * lev_dev
    tall = jnp.where(
        (row == mine) | (row == mine + 1), jnp.broadcast_to(coup[...], (depth, lev_dev)), tall
    )
    tall = tall.astype(BF)
    row = iota((lev_dev, 2 * BLK), 0)
    col = iota((lev_dev, 2 * BLK), 1)
    odd = iota((depth, 2 * BLK), 0) & 1
    right = (iota((depth, 2 * BLK), 1) >= BLK).astype(jnp.int32)
    for t in range(3):
        onto = jnp.where((col & (BLK - 1)) == row + t * KP, 1.0, 0.0).astype(BF)
        spread_out = jnp.dot(tall, onto, preferred_element_type=F32)
        wide[t] = jnp.where(odd == right, spread_out, 0.0).astype(BF)

    load_idx.wait()
    load_wgt.wait()
    blocks = idx.shape[0]
    build_spread(idx, wgt, spread, 0, blocks - LATE)

    for c in range(len(CHUNKS)):
        for i in range(1, nl):
            copy_a(i, c).wait()
    size = Q * lat
    lane = iota((size, BLK), 1)
    for i in range(1, nl):
        v = lax.rem(lev + i, nl)
        last = gall[v, 2 * size : 3 * size, :]
        full[v, 4 * size : 5 * size, :] = last
        last = last.astype(F32)
        for c in range(2):
            pair = gall[v, c * size : (c + 1) * size, :]
            full[v, 2 * c * size : (2 * c + 1) * size, :] = pair
            end = pltpu.roll(last, 2 * BLK + used - tail - spare - c * tail - BLK, 1)
            pair = jnp.where(lane < used - tail, pltpu.roll(pair.astype(F32), BLK - used, 1), end)
            full[v, (2 * c + 1) * size : (2 * c + 2) * size, :] = pair.astype(BF)

    group = 16
    pairs = group // 2

    def hydro(g):
        parts = []
        for k in range(BLOCKS):
            at = k * Q * lat + g * Q * group
            at = at if isinstance(at, int) else pl.multiple_of(at, 16)
            parts.append(pl.ds(at, Q * group))
        left = jnp.concatenate(
            [jnp.concatenate([full[v, p] for v in range(nl)], axis=1) for p in parts], axis=0
        )
        result = []
        for t in range(3):
            value = jnp.dot(left, wide[t], preferred_element_type=F32)
            value = value.reshape(BLOCKS, pairs, 2 * Q, 2 * BLK)
            result.append([value[:, p].reshape(PR, 2 * BLK) for p in range(pairs)])
        return result

    def pack(b, value):
        value = jnp.concatenate([value[:, :BLK], value[:, BLK:]], axis=0)
        pieces[b] = value.astype(BF)

    if lat == group:
        result = hydro(0)
        for b in range(nb):
            value = result[1][b]
            for t in (0, 2):
                if 0 <= b - 1 + t < pairs:
                    value = value + result[t][b - 1 + t]
            pack(b, value)
    else:
        total[...] = jnp.zeros_like(total)

        def many(g, _):
            result = hydro(g)
            for t in range(3):
                for p in range(pairs):
                    place = g * pairs + p + 2 - t
                    total[place] = total[place] + result[t][p]
            return 0

        def finish(b, _):
            pack(b, total[b + 1])
            return 0

        lax.fori_loop(0, lat // group, many, 0)
        lax.fori_loop(0, nb, finish, 0)

    def copy_b(i):
        peer = lax.rem(band + i, nb)
        return pltpu.make_async_remote_copy(
            src_ref=pieces.at[peer],
            dst_ref=out_ref.at[band],
            send_sem=sb.at[i],
            recv_sem=rb.at[i],
            device_id=(peer, lev),
            device_id_type=MESH,
        )

    def send(i, _):
        copy_b(i).start()
        return 0

    lax.fori_loop(1, nb, send, 0)
    out_ref[band] = pieces[band]
    build_spread(idx, wgt, spread, blocks - LATE, blocks)
    if early:
        build_table(m_ref, table, nb)

    def done(i, _):
        copy_b(i).wait()
        return 0

    lax.fori_loop(1, nb, done, 0)


def exchange(temp, surf, legendre, m_order, hydro, coupling, idx, wgt, nb, nl, early):
    _, lev_dev, _, width = temp.shape
    lat = legendre.shape[1]
    blocks = idx.shape[0]
    vmem = pl.BlockSpec(memory_space=pltpu.VMEM)
    hbm = pl.BlockSpec(memory_space=pltpu.HBM)
    out_shape = [
        jax.ShapeDtypeStruct((nb, 2 * PR, BLK), BF),
        jax.ShapeDtypeStruct((blocks, 2 * HALF, BLK), BF),
    ]
    if early:
        out_shape.append(jax.ShapeDtypeStruct((nb * PR, NLON), BF))
    return pl.pallas_call(
        functools.partial(exchange_kernel, nb, nl, lat, lev_dev, early),
        out_shape=out_shape,
        in_specs=[hbm] * 8,
        out_specs=[vmem] * len(out_shape),
        scratch_shapes=[
            pltpu.VMEM((S, lev_dev + 1, 2, width), BF),
            pltpu.VMEM(legendre.shape, BF),
            pltpu.VMEM(hydro.shape, BF),
            pltpu.VMEM(coupling.shape, F32),
            pltpu.VMEM(idx.shape, jnp.int32),
            pltpu.VMEM(wgt.shape, F32),
            pltpu.SMEM(m_order.shape, jnp.int32),
            pltpu.VMEM((BLOCKS + len(CHUNKS), Q * lat, BLK), F32),
            pltpu.VMEM((nl, len(CHUNKS) * Q * lat, BLK), BF),
            pltpu.VMEM((nl, S * lat, BLK), BF),
            pltpu.VMEM((3, nl * BLK, 2 * BLK), BF),
            pltpu.VMEM((nb + 2 if lat > 16 else 1, PR, 2 * BLK), F32),
            pltpu.VMEM((nb, 2 * PR, BLK), BF),
            pltpu.SemaphoreType.DMA((2 * len(CHUNKS),)),
            pltpu.SemaphoreType.DMA((6,)),
            pltpu.SemaphoreType.DMA((len(CHUNKS) * nl,)),
            pltpu.SemaphoreType.DMA((len(CHUNKS) * nl,)),
            pltpu.SemaphoreType.DMA((nb,)),
            pltpu.SemaphoreType.DMA((nb,)),
        ],
        compiler_params=pltpu.CompilerParams(
            collective_id=0, has_side_effects=True, vmem_limit_bytes=(30 if early else 52) * 1024 * 1024
        ),
    )(*[
        pltpu.with_memory_space_constraint(x, pltpu.HBM)
        for x in (temp, surf, legendre, m_order, hydro, coupling, idx, wgt)
    ])


def grid_kernel(nb, lev_dev, early, src_ref, coef_ref, spread, *refs):
    if early:
        table, out_ref, src, pool, grid, ss, so = refs
    else:
        m_ref, out_ref, src, pool, grid, ss, so, table = refs
        build_table(m_ref, table, nb)
    load_src = pltpu.make_async_copy(src_ref, src, ss)
    load_src.start()
    coef = coef_ref[...].astype(F32)
    left = []
    for p in range(2):
        tiles = []
        for b in range(nb):
            value = coef[b]
            for r, k in [(r, k) for r in range(2) for k in range(4)] + [(0, 4), (1, 4)]:
                at = r * PR + k * 2 * Q + p * Q
                tiles.append(value[at : at + Q])
        left.append(jnp.concatenate(tiles, axis=0).T)
    left = jnp.concatenate(left, axis=0).astype(BF)
    group = 4

    def synth(c, _):
        cols = pl.ds(pl.multiple_of(c * (group * BLK), 128), group * BLK)
        value = jnp.dot(left, table[:, cols], preferred_element_type=F32).astype(BF)
        for t in range(3):
            for p in range(2):
                at = p * BLK + t * KP
                for g in range(group):
                    pool[(2 * t + p) * XB + c * group + g] = value[
                        at : at + KP, g * BLK : (g + 1) * BLK
                    ]
        return 0

    lax.fori_loop(0, XB // group, synth, 0, unroll=XB // group if early else 1)
    load_src.wait()

    first = (lax.axis_index("band") - 1) * (2 * XB)

    def read(b):
        source = jnp.concatenate([pool[src[i, b] - first] for i in range(4)], axis=1)
        return jnp.dot(source, spread[b], preferred_element_type=F32)

    def write(q):
        cols = pl.ds(q * (STEP * BLK), STEP * BLK)
        return pltpu.make_async_copy(grid.at[:, :, cols], out_ref.at[:, :, cols], so.at[q])

    for q in range(XB // STEP):
        for x in range(q * STEP, (q + 1) * STEP):
            for j in range(2):
                grid[:, j, x * BLK : (x + 1) * BLK] = read(j * XB + x)[:lev_dev]
        write(q).start()
    for q in range(XB // STEP):
        write(q).wait()


def grid_part(src, m_order, coef, spread, table, nb, lev_dev):
    vmem = pl.BlockSpec(memory_space=pltpu.VMEM)
    hbm = pl.BlockSpec(memory_space=pltpu.HBM)
    early = len(table) > 0
    scratch = [
        pltpu.SMEM(src.shape, jnp.int32),
        pltpu.VMEM((JJ * XB, KP, BLK), BF),
        pltpu.VMEM((lev_dev, 2, NLON), F32),
        pltpu.SemaphoreType.DMA,
        pltpu.SemaphoreType.DMA((XB // STEP,)),
    ]
    src = pltpu.with_memory_space_constraint(src, pltpu.HBM)
    if early:
        last, specs = list(table), [vmem]
    else:
        last, specs = [m_order], [pl.BlockSpec(memory_space=pltpu.SMEM)]
        scratch.append(pltpu.VMEM((nb * PR, NLON), BF))
    return pl.pallas_call(
        functools.partial(grid_kernel, nb, lev_dev, early),
        out_shape=jax.ShapeDtypeStruct((lev_dev, 2, NLON), F32),
        in_specs=[hbm, vmem, vmem] + specs,
        out_specs=hbm,
        scratch_shapes=scratch,
        compiler_params=pltpu.CompilerParams(
            vmem_limit_bytes=(24 if early else 54) * 1024 * 1024
        ),
    )(src, coef, spread, *last)


def shards(
    temp_spectrum,
    surf_spectrum,
    legendre,
    m_order,
    hydro_matrix,
    surf_coupling,
    src_blocks,
    tap_index,
    tap_weight,
):
    lev_dev = temp_spectrum.shape[3]
    nb, nl = lax.axis_size("band"), lax.axis_size("lev")
    early = nb <= 16
    coef, spread, *table = exchange(
        jnp.transpose(temp_spectrum, (0, 3, 2, 1)),
        jnp.transpose(surf_spectrum, (0, 2, 1)),
        legendre,
        m_order,
        hydro_matrix,
        surf_coupling[None, :],
        tap_index,
        tap_weight,
        nb,
        nl,
        early,
    )
    out = grid_part(src_blocks.T, m_order, coef, spread, table, nb, lev_dev)
    return jnp.transpose(out, (1, 0, 2))


def solution(mesh):
    in_specs = (
        P("band", None, None, "lev"),
        P("band", None, None),
        P("band", None, None),
        P(),
        P("lev", None),
        P("lev"),
        P("band", None),
        P("band", None, None),
        P("band", None, None),
    )
    out_specs = P("band", "lev", None)
    return jax.shard_map(shards, mesh=mesh, in_specs=in_specs, out_specs=out_specs, check_vma=False)
```

```python
import functools
import math

import jax
import jax.numpy as jnp
from jax import lax
from jax.experimental import pallas as pl
from jax.experimental.pallas import tpu as pltpu
from jax.sharding import PartitionSpec as P

NLON = 5120
BLK = 128
TAPS = 4
XB = NLON // BLK
S = 20
CHUNKS = ((0, 8), (8, 8), (16, 4))
Q = 4
BLOCKS = S // Q
KP = 40
PR = 40
JJ = 6
HALF = 256
LATE = 46
STEP = 5
MESH = pl.DeviceIdType.MESH
BF = jnp.bfloat16
F32 = jnp.float32


def iota(shape, dim):
    return lax.broadcasted_iota(jnp.int32, shape, dim)


def cosine(steps):
    steps = steps - NLON * jnp.floor(steps * (1.0 / NLON))
    y = (jnp.abs(steps * (1.0 / NLON) - 0.5) - 0.25) * (2.0 * math.pi)
    z = y * y
    p = -1.0 / 39916800.0
    for c in (1.0 / 362880.0, -1.0 / 5040.0, 1.0 / 120.0, -1.0 / 6.0, 1.0):
        p = p * z + c
    return y * p


def table_rows(m_ref, table, pair):
    row = iota((8, BLK), 0)
    point = iota((8, BLK), 1).astype(F32)
    first, second, turns = [], [], []
    for u in range(2):
        base = (pair * 2 + u) * S
        orders = []
        for start, count in CHUNKS:
            tile = jnp.zeros((8, BLK), F32)
            for i in range(8):
                value = m_ref[base + start + i % count].astype(F32)
                tile = jnp.where(row == i, value, tile)
            orders.append(tile)
        turn = [2.0 * cosine(o * float(BLK)) for o in orders]
        shift = jnp.where(row >= 4, NLON // 4, 0).astype(F32)
        for c, s in ((0, 0.0), (1, 0.0), (0, NLON / 4), (1, NLON / 4), (2, shift)):
            factor = jnp.where(orders[c] == 0.0, 1.0, 2.0)
            first.append(factor * cosine(orders[c] * point + s))
            second.append(factor * cosine(orders[c] * (point + float(BLK)) + s))
            turns.append(turn[c])
    old = jnp.concatenate(first, axis=0)
    new = jnp.concatenate(second, axis=0)
    turn = jnp.concatenate(turns, axis=0)
    place = pl.ds(pl.multiple_of(pair * 2 * PR, 16), 2 * PR)
    for x in range(XB):
        table[place, x * BLK : (x + 1) * BLK] = old.astype(BF)
        old, new = new, turn * new - old


def build_table(m_ref, table, nb):
    def pair(b, _):
        table_rows(m_ref, table, b)
        return 0

    lax.fori_loop(0, nb // 2, pair, 0)


def build_spread(idx, wgt, spread, first, last):
    cells = iota((HALF, BLK), 0).astype(BF)
    zero = jnp.zeros((HALF, BLK), BF)

    def block(b, _):
        index = idx[b]
        weight = wgt[b].astype(BF)
        for h in range(2):
            spot = (index - h * HALF).astype(F32).astype(BF)
            total = None
            for t in range(TAPS):
                hit = cells == jnp.broadcast_to(spot[t : t + 1, :], (HALF, BLK))
                part = jnp.where(hit, jnp.broadcast_to(weight[t : t + 1, :], (HALF, BLK)), zero)
                total = part if total is None else total + part
            spread[b, h * HALF : (h + 1) * HALF, :] = total
        return 0

    lax.fori_loop(first, last, block, 0)


def exchange_kernel(
    nb, nl, lat, lev_dev, early, *refs
):
    (temp_ref, surf_ref, leg_ref, ord_ref, h_ref, c_ref, idx_ref, wgt_ref), refs = refs[:8], refs[8:]
    out_ref, spread = refs[:2]
    table = refs[2] if early else None
    refs = refs[2 + early :]
    (buf, leg, h, coup, idx, wgt, m_ref, rows, gall, full, wide, total, pieces) = refs[:13]
    (sl, sm, sa, ra, sb, rb) = refs[13:]
    band = lax.axis_index("band")
    lev = lax.axis_index("lev")
    chunks = len(CHUNKS)

    def load_temp(c):
        part = pl.ds(*CHUNKS[c])
        return pltpu.make_async_copy(temp_ref.at[part], buf.at[part, pl.ds(0, lev_dev)], sl.at[c])

    def load_leg(c):
        part = pl.ds(*CHUNKS[c])
        return pltpu.make_async_copy(leg_ref.at[part], leg.at[part], sl.at[chunks + c])

    load_surf = pltpu.make_async_copy(surf_ref, buf.at[:, lev_dev], sm.at[0])
    load_again = pltpu.make_async_copy(surf_ref, buf.at[:, lev_dev + 1], sm.at[6])
    load_h = pltpu.make_async_copy(h_ref, h, sm.at[1])
    load_c = pltpu.make_async_copy(c_ref, coup, sm.at[2])
    load_idx = pltpu.make_async_copy(idx_ref, idx, sm.at[3])
    load_wgt = pltpu.make_async_copy(wgt_ref, wgt, sm.at[4])
    load_m = pltpu.make_async_copy(ord_ref, m_ref, sm.at[5])
    load_m.start()
    load_surf.start()
    load_again.start()
    load_leg(0).start()
    load_temp(0).start()

    barrier = pltpu.get_barrier_semaphore()

    def greet_lev(i, _):
        pl.semaphore_signal(
            barrier, inc=1, device_id=(band, lax.rem(lev + i, nl)), device_id_type=MESH
        )
        return 0

    def greet_band(i, _):
        pl.semaphore_signal(
            barrier, inc=1, device_id=(lax.rem(band + i, nb), lev), device_id_type=MESH
        )
        return 0

    lax.fori_loop(1, nb, greet_band, 0)
    lax.fori_loop(1, nl, greet_lev, 0)
    for c in range(1, chunks):
        load_leg(c).start()
        load_temp(c).start()
    load_h.start()
    load_c.start()
    load_idx.start()
    load_wgt.start()

    def copy_a(i, c):
        part = pl.ds(c * Q * lat, Q * lat)
        return pltpu.make_async_remote_copy(
            src_ref=gall.at[lev, part],
            dst_ref=gall.at[lev, part],
            send_sem=sa.at[c * nl + i],
            recv_sem=ra.at[c * nl + i],
            device_id=(band, lax.rem(lev + i, nl)),
            device_id_type=MESH,
        )

    width = leg_ref.shape[2]
    used = 2 * lev_dev
    tail = 2 * used - BLK
    spare = used + 4
    order = iota((lat, width), 1)
    lane = iota((lat, BLK), 1)
    blank = jnp.zeros((lat, BLK - used - 4), F32)

    def transform(s):
        m = m_ref[band * S + s]
        keep = jnp.where(order >= m, 1.0, 0.0).astype(BF)
        coef = buf[s].reshape(used + 4, width)
        four = lax.dot_general(
            leg[s] * keep, coef, (((1,), (1,)), ((), ())), preferred_element_type=F32
        )
        return jnp.concatenate([four, blank], axis=1)

    def place(block, q, value):
        rows[block, pl.ds(q, lat, stride=Q), :] = value

    load_m.wait()
    load_surf.wait()
    load_again.wait()
    ends = [None] * Q
    for c, (start, count) in enumerate(CHUNKS):
        load_leg(c).wait()
        load_temp(c).wait()
        for q in range(Q):
            one = transform(start + q)
            place(start // Q, q, one)
            if count == 2 * Q:
                two = transform(start + Q + q)
                place(start // Q + 1, q, two)
                place(BLOCKS + c, q, jnp.where(lane < used, one, pltpu.roll(two, used, 1)))
                end = pltpu.roll(two, spare + c * tail - used + tail, 1)
                ends[q] = end if c == 0 else jnp.where(lane < spare + c * tail, ends[q], end)
            else:
                place(BLOCKS + c, q, jnp.where(lane < used, one, ends[q]))
        gall[lev, c * Q * lat : (c + 1) * Q * lat, :] = rows[BLOCKS + c].astype(BF)
        if c == 0:
            pl.semaphore_wait(barrier, nl - 1 + nb - 1)
        for i in range(1, nl):
            copy_a(i, c).start()
    for k in range(BLOCKS):
        full[lev, k * Q * lat : (k + 1) * Q * lat, :] = rows[k].astype(BF)

    depth = nl * BLK
    lev_total = h_ref.shape[1]
    load_h.wait()
    load_c.wait()
    row = iota((lev_dev, lev_total), 0) + lev * lev_dev
    col = iota((lev_dev, lev_total), 1)
    upper = jnp.where(col >= row, h[...].astype(F32), 0.0).astype(BF)
    row = iota((depth, lev_total), 0)
    col = iota((depth, lev_total), 1)
    spots = jnp.zeros((depth, lev_total), F32)
    for v in range(nl):
        step = row - v * BLK - 2 * (col - v * lev_dev)
        inside = (col >= v * lev_dev) & (col < (v + 1) * lev_dev)
        spots = jnp.where(inside & (step >= 0) & (step < 2), 1.0, spots)
    tall = lax.dot_general(
        spots.astype(BF), upper, (((1,), (1,)), ((), ())), preferred_element_type=F32
    )
    row = iota((depth, lev_dev), 0)
    mine = lev * BLK + 2 * lev_dev
    high = coup[...].astype(BF).astype(F32)
    tall = jnp.where(
        (row == mine) | (row == mine + 1), jnp.broadcast_to(high, (depth, lev_dev)), tall
    )
    tall = jnp.where(
        (row == mine + 2) | (row == mine + 3),
        jnp.broadcast_to(coup[...] - high, (depth, lev_dev)),
        tall,
    )
    tall = tall.astype(BF)
    row = iota((lev_dev, 2 * BLK), 0)
    col = iota((lev_dev, 2 * BLK), 1)
    odd = iota((depth, 2 * BLK), 0) & 1
    right = (iota((depth, 2 * BLK), 1) >= BLK).astype(jnp.int32)
    for t in range(3):
        onto = jnp.where((col & (BLK - 1)) == row + t * KP, 1.0, 0.0).astype(BF)
        spread_out = jnp.dot(tall, onto, preferred_element_type=F32)
        wide[t] = jnp.where(odd == right, spread_out, 0.0).astype(BF)

    load_idx.wait()
    load_wgt.wait()
    blocks = idx.shape[0]
    build_spread(idx, wgt, spread, 0, blocks - LATE)

    for c in range(len(CHUNKS)):
        for i in range(1, nl):
            copy_a(i, c).wait()
    size = Q * lat
    lane = iota((size, BLK), 1)
    for i in range(1, nl):
        v = lax.rem(lev + i, nl)
        last = gall[v, 2 * size : 3 * size, :]
        full[v, 4 * size : 5 * size, :] = last
        last = last.astype(F32)
        for c in range(2):
            pair = gall[v, c * size : (c + 1) * size, :]
            full[v, 2 * c * size : (2 * c + 1) * size, :] = pair
            end = pltpu.roll(last, 2 * BLK + used - tail - spare - c * tail - BLK, 1)
            pair = jnp.where(lane < used - tail, pltpu.roll(pair.astype(F32), BLK - used, 1), end)
            full[v, (2 * c + 1) * size : (2 * c + 2) * size, :] = pair.astype(BF)

    group = 16
    pairs = group // 2

    def hydro(g):
        parts = []
        for k in range(BLOCKS):
            at = k * Q * lat + g * Q * group
            at = at if isinstance(at, int) else pl.multiple_of(at, 16)
            parts.append(pl.ds(at, Q * group))
        left = jnp.concatenate(
            [jnp.concatenate([full[v, p] for v in range(nl)], axis=1) for p in parts], axis=0
        )
        result = []
        for t in range(3):
            value = jnp.dot(left, wide[t], preferred_element_type=F32)
            value = value.reshape(BLOCKS, pairs, 2 * Q, 2 * BLK)
            result.append([value[:, p].reshape(PR, 2 * BLK) for p in range(pairs)])
        return result

    def pack(b, value):
        value = jnp.concatenate([value[:, :BLK], value[:, BLK:]], axis=0)
        pieces[b] = value.astype(BF)

    if lat == group:
        result = hydro(0)
        for b in range(nb):
            value = result[1][b]
            for t in (0, 2):
                if 0 <= b - 1 + t < pairs:
                    value = value + result[t][b - 1 + t]
            pack(b, value)
    else:
        total[...] = jnp.zeros_like(total)

        def many(g, _):
            result = hydro(g)
            for t in range(3):
                for p in range(pairs):
                    place = g * pairs + p + 2 - t
                    total[place] = total[place] + result[t][p]
            return 0

        def finish(b, _):
            pack(b, total[b + 1])
            return 0

        lax.fori_loop(0, lat // group, many, 0)
        lax.fori_loop(0, nb, finish, 0)

    def copy_b(i):
        peer = lax.rem(band + i, nb)
        return pltpu.make_async_remote_copy(
            src_ref=pieces.at[peer],
            dst_ref=out_ref.at[band],
            send_sem=sb.at[i],
            recv_sem=rb.at[i],
            device_id=(peer, lev),
            device_id_type=MESH,
        )

    def send(i, _):
        copy_b(i).start()
        return 0

    lax.fori_loop(1, nb, send, 0)
    out_ref[band] = pieces[band]
    build_spread(idx, wgt, spread, blocks - LATE, blocks)
    if early:
        build_table(m_ref, table, nb)

    def done(i, _):
        copy_b(i).wait()
        return 0

    lax.fori_loop(1, nb, done, 0)


def exchange(temp, surf, legendre, m_order, hydro, coupling, idx, wgt, nb, nl, early):
    _, lev_dev, _, width = temp.shape
    lat = legendre.shape[1]
    blocks = idx.shape[0]
    vmem = pl.BlockSpec(memory_space=pltpu.VMEM)
    hbm = pl.BlockSpec(memory_space=pltpu.HBM)
    out_shape = [
        jax.ShapeDtypeStruct((nb, 2 * PR, BLK), BF),
        jax.ShapeDtypeStruct((blocks, 2 * HALF, BLK), BF),
    ]
    if early:
        out_shape.append(jax.ShapeDtypeStruct((nb * PR, NLON), BF))
    return pl.pallas_call(
        functools.partial(exchange_kernel, nb, nl, lat, lev_dev, early),
        out_shape=out_shape,
        in_specs=[hbm] * 8,
        out_specs=[vmem] * len(out_shape),
        scratch_shapes=[
            pltpu.VMEM((S, lev_dev + 2, 2, width), BF),
            pltpu.VMEM(legendre.shape, BF),
            pltpu.VMEM(hydro.shape, BF),
            pltpu.VMEM(coupling.shape, F32),
            pltpu.VMEM(idx.shape, jnp.int32),
            pltpu.VMEM(wgt.shape, F32),
            pltpu.SMEM(m_order.shape, jnp.int32),
            pltpu.VMEM((BLOCKS + len(CHUNKS), Q * lat, BLK), F32),
            pltpu.VMEM((nl, len(CHUNKS) * Q * lat, BLK), BF),
            pltpu.VMEM((nl, S * lat, BLK), BF),
            pltpu.VMEM((3, nl * BLK, 2 * BLK), BF),
            pltpu.VMEM((nb + 2 if lat > 16 else 1, PR, 2 * BLK), F32),
            pltpu.VMEM((nb, 2 * PR, BLK), BF),
            pltpu.SemaphoreType.DMA((2 * len(CHUNKS),)),
            pltpu.SemaphoreType.DMA((7,)),
            pltpu.SemaphoreType.DMA((len(CHUNKS) * nl,)),
            pltpu.SemaphoreType.DMA((len(CHUNKS) * nl,)),
            pltpu.SemaphoreType.DMA((nb,)),
            pltpu.SemaphoreType.DMA((nb,)),
        ],
        compiler_params=pltpu.CompilerParams(
            collective_id=0, has_side_effects=True, vmem_limit_bytes=(30 if early else 52) * 1024 * 1024
        ),
    )(*[
        pltpu.with_memory_space_constraint(x, pltpu.HBM)
        for x in (temp, surf, legendre, m_order, hydro, coupling, idx, wgt)
    ])


def grid_kernel(nb, lev_dev, early, src_ref, coef_ref, spread, *refs):
    if early:
        table, out_ref, src, pool, grid, ss, so = refs
    else:
        m_ref, out_ref, src, pool, grid, ss, so, table = refs
        build_table(m_ref, table, nb)
    load_src = pltpu.make_async_copy(src_ref, src, ss)
    load_src.start()
    coef = coef_ref[...].astype(F32)
    left = []
    for p in range(2):
        tiles = []
        for b in range(nb):
            value = coef[b]
            for r, k in [(r, k) for r in range(2) for k in range(4)] + [(0, 4), (1, 4)]:
                at = r * PR + k * 2 * Q + p * Q
                tiles.append(value[at : at + Q])
        left.append(jnp.concatenate(tiles, axis=0).T)
    left = jnp.concatenate(left, axis=0).astype(BF)
    group = 4

    def synth(c, _):
        cols = pl.ds(pl.multiple_of(c * (group * BLK), 128), group * BLK)
        value = jnp.dot(left, table[:, cols], preferred_element_type=F32).astype(BF)
        for t in range(3):
            for p in range(2):
                at = p * BLK + t * KP
                for g in range(group):
                    pool[(2 * t + p) * XB + c * group + g] = value[
                        at : at + KP, g * BLK : (g + 1) * BLK
                    ]
        return 0

    lax.fori_loop(0, XB // group, synth, 0, unroll=XB // group if early else 1)
    load_src.wait()

    first = (lax.axis_index("band") - 1) * (2 * XB)

    def read(b):
        source = jnp.concatenate([pool[src[i, b] - first] for i in range(4)], axis=1)
        return jnp.dot(source, spread[b], preferred_element_type=F32)

    def write(q):
        cols = pl.ds(q * (STEP * BLK), STEP * BLK)
        return pltpu.make_async_copy(grid.at[:, :, cols], out_ref.at[:, :, cols], so.at[q])

    for q in range(XB // STEP):
        for x in range(q * STEP, (q + 1) * STEP):
            for j in range(2):
                grid[:, j, x * BLK : (x + 1) * BLK] = read(j * XB + x)[:lev_dev]
        write(q).start()
    for q in range(XB // STEP):
        write(q).wait()


def grid_part(src, m_order, coef, spread, table, nb, lev_dev):
    vmem = pl.BlockSpec(memory_space=pltpu.VMEM)
    hbm = pl.BlockSpec(memory_space=pltpu.HBM)
    early = len(table) > 0
    scratch = [
        pltpu.SMEM(src.shape, jnp.int32),
        pltpu.VMEM((JJ * XB, KP, BLK), BF),
        pltpu.VMEM((lev_dev, 2, NLON), F32),
        pltpu.SemaphoreType.DMA,
        pltpu.SemaphoreType.DMA((XB // STEP,)),
    ]
    src = pltpu.with_memory_space_constraint(src, pltpu.HBM)
    if early:
        last, specs = list(table), [vmem]
    else:
        last, specs = [m_order], [pl.BlockSpec(memory_space=pltpu.SMEM)]
        scratch.append(pltpu.VMEM((nb * PR, NLON), BF))
    return pl.pallas_call(
        functools.partial(grid_kernel, nb, lev_dev, early),
        out_shape=jax.ShapeDtypeStruct((lev_dev, 2, NLON), F32),
        in_specs=[hbm, vmem, vmem] + specs,
        out_specs=hbm,
        scratch_shapes=scratch,
        compiler_params=pltpu.CompilerParams(
            vmem_limit_bytes=(24 if early else 54) * 1024 * 1024
        ),
    )(src, coef, spread, *last)


def shards(
    temp_spectrum,
    surf_spectrum,
    legendre,
    m_order,
    hydro_matrix,
    surf_coupling,
    src_blocks,
    tap_index,
    tap_weight,
):
    lev_dev = temp_spectrum.shape[3]
    nb, nl = lax.axis_size("band"), lax.axis_size("lev")
    early = nb <= 16
    coef, spread, *table = exchange(
        jnp.transpose(temp_spectrum, (0, 3, 2, 1)),
        jnp.transpose(surf_spectrum, (0, 2, 1)),
        legendre,
        m_order,
        hydro_matrix,
        surf_coupling[None, :],
        tap_index,
        tap_weight,
        nb,
        nl,
        early,
    )
    out = grid_part(src_blocks.T, m_order, coef, spread, table, nb, lev_dev)
    return jnp.transpose(out, (1, 0, 2))


def solution(mesh):
    in_specs = (
        P("band", None, None, "lev"),
        P("band", None, None),
        P("band", None, None),
        P(),
        P("lev", None),
        P("lev"),
        P("band", None),
        P("band", None, None),
        P("band", None, None),
    )
    out_specs = P("band", "lev", None)
    return jax.shard_map(shards, mesh=mesh, in_specs=in_specs, out_specs=out_specs, check_vma=False)
```

```python
import functools
import math

import jax
import jax.numpy as jnp
from jax import lax
from jax.experimental import pallas as pl
from jax.experimental.pallas import tpu as pltpu
from jax.sharding import PartitionSpec as P

NLON = 5120
BLK = 128
TAPS = 4
XB = NLON // BLK
XH = XB // 2
HALF_LON = NLON // 2
S = 20
CHUNKS = ((0, 8), (8, 8), (16, 4))
Q = 4
BLOCKS = S // Q
KP = 40
PR = 40
JJ = 6
HALF = 256
WORK = (10, 40, 30, 0)
STEP = 5
MESH = pl.DeviceIdType.MESH
BF = jnp.bfloat16
F32 = jnp.float32


def iota(shape, dim):
    return lax.broadcasted_iota(jnp.int32, shape, dim)


def cosine(steps):
    steps = steps - NLON * jnp.floor(steps * (1.0 / NLON))
    y = (jnp.abs(steps * (1.0 / NLON) - 0.5) - 0.25) * (2.0 * math.pi)
    z = y * y
    p = -1.0 / 39916800.0
    for c in (1.0 / 362880.0, -1.0 / 5040.0, 1.0 / 120.0, -1.0 / 6.0, 1.0):
        p = p * z + c
    return y * p


def table_rows(m_ref, table, signs, pair):
    row = iota((8, BLK), 0)
    point = iota((8, BLK), 1).astype(F32)
    first, second, turns, parity = [], [], [], []
    for u in range(2):
        base = (pair * 2 + u) * S
        orders = []
        for start, count in CHUNKS:
            tile = jnp.zeros((8, BLK), F32)
            for i in range(8):
                value = m_ref[base + start + i % count].astype(F32)
                tile = jnp.where(row == i, value, tile)
            orders.append(tile)
        turn = [2.0 * cosine(o * float(BLK)) for o in orders]
        shift = jnp.where(row >= 4, NLON // 4, 0).astype(F32)
        for c, s in ((0, 0.0), (1, 0.0), (0, NLON / 4), (1, NLON / 4), (2, shift)):
            factor = jnp.where(orders[c] == 0.0, 1.0, 2.0)
            first.append(factor * cosine(orders[c] * point + s))
            second.append(factor * cosine(orders[c] * (point + float(BLK)) + s))
            turns.append(turn[c])
            half = orders[c] * 0.5
            parity.append(1.0 - 4.0 * (half - jnp.floor(half)))
    old = jnp.concatenate(first, axis=0)
    new = jnp.concatenate(second, axis=0)
    turn = jnp.concatenate(turns, axis=0)
    place = pl.ds(pl.multiple_of(pair * 2 * PR, 16), 2 * PR)
    signs[place, :] = jnp.concatenate(parity, axis=0)
    for x in range(XH):
        table[place, x * BLK : (x + 1) * BLK] = old.astype(BF)
        old, new = new, turn * new - old


def build_table(m_ref, table, signs, nb):
    def pair(b, _):
        table_rows(m_ref, table, signs, b)
        return 0

    lax.fori_loop(0, nb // 2, pair, 0)


def build_spread(idx, wgt, spread, first, last):
    cells = iota((HALF, BLK), 0).astype(BF)
    zero = jnp.zeros((HALF, BLK), BF)

    def block(b, _):
        index = idx[b]
        weight = wgt[b].astype(BF)
        for h in range(2):
            spot = (index - h * HALF).astype(F32).astype(BF)
            total = None
            for t in range(TAPS):
                hit = cells == jnp.broadcast_to(spot[t : t + 1, :], (HALF, BLK))
                part = jnp.where(hit, jnp.broadcast_to(weight[t : t + 1, :], (HALF, BLK)), zero)
                total = part if total is None else total + part
            spread[b, h * HALF : (h + 1) * HALF, :] = total
        return 0

    lax.fori_loop(first, last, block, 0)


def assemble(coef, sign):
    left = []
    for p in range(2):
        tiles = []
        for b in range(coef.shape[0]):
            value = coef[b].astype(F32)
            for r, k in [(r, k) for r in range(2) for k in range(4)] + [(0, 4), (1, 4)]:
                at = r * PR + k * 2 * Q + p * Q
                tiles.append(value[at : at + Q])
        left.append(jnp.concatenate(tiles, axis=0).T)
    left = jnp.concatenate(left, axis=0)
    return jnp.concatenate([left, left * sign], axis=0).astype(BF)


def halves(band, nb):
    half = nb // 2
    near = (band // half) * half
    return half, near, lax.rem(near + half, nb)


def table_part(table, start, half, cols):
    return table[pl.ds(pl.multiple_of(start * PR, 16), half * PR), cols]


def exchange_kernel(
    nb, nl, lat, lev_dev, early, *refs
):
    (temp_ref, surf_ref, leg_ref, ord_ref, h_ref, c_ref, idx_ref, wgt_ref), refs = refs[:8], refs[8:]
    out_ref, spread = refs[:2]
    if early:
        table, partial, sign = refs[2:5]
    refs = refs[2 + 3 * early :]
    (buf, leg, h, coup, idx, wgt, m_ref, rows, gall, full, wide, total, pieces, signs) = refs[:14]
    (sl, sm, sa, ra, sb, rb) = refs[14:]
    band = lax.axis_index("band")
    lev = lax.axis_index("lev")
    chunks = len(CHUNKS)

    def load_temp(c):
        part = pl.ds(*CHUNKS[c])
        return pltpu.make_async_copy(temp_ref.at[part], buf.at[part, pl.ds(0, lev_dev)], sl.at[c])

    def load_leg(c):
        part = pl.ds(*CHUNKS[c])
        return pltpu.make_async_copy(leg_ref.at[part], leg.at[part], sl.at[chunks + c])

    load_surf = pltpu.make_async_copy(surf_ref, buf.at[:, lev_dev], sm.at[0])
    load_again = pltpu.make_async_copy(surf_ref, buf.at[:, lev_dev + 1], sm.at[6])
    load_h = pltpu.make_async_copy(h_ref, h, sm.at[1])
    load_c = pltpu.make_async_copy(c_ref, coup, sm.at[2])
    load_idx = pltpu.make_async_copy(idx_ref, idx, sm.at[3])
    load_wgt = pltpu.make_async_copy(wgt_ref, wgt, sm.at[4])
    load_m = pltpu.make_async_copy(ord_ref, m_ref, sm.at[5])
    load_idx.start()
    load_wgt.start()
    load_m.start()
    load_surf.start()
    load_again.start()
    load_leg(0).start()
    load_temp(0).start()

    barrier = pltpu.get_barrier_semaphore()

    def greet_lev(i, _):
        pl.semaphore_signal(
            barrier, inc=1, device_id=(band, lax.rem(lev + i, nl)), device_id_type=MESH
        )
        return 0

    def greet_band(i, _):
        pl.semaphore_signal(
            barrier, inc=1, device_id=(lax.rem(band + i, nb), lev), device_id_type=MESH
        )
        return 0

    lax.fori_loop(1, nb, greet_band, 0)
    lax.fori_loop(1, nl, greet_lev, 0)
    for c in range(1, chunks):
        load_leg(c).start()
        load_temp(c).start()
    load_h.start()
    load_c.start()
    load_idx.wait()
    load_wgt.wait()
    marks = [0]
    for count in WORK:
        marks.append(marks[-1] + count)
    assert marks[-1] == idx.shape[0]

    def build(part):
        build_spread(idx, wgt, spread, marks[part], marks[part + 1])

    build(0)

    def copy_a(i, c):
        part = pl.ds(c * Q * lat, Q * lat)
        return pltpu.make_async_remote_copy(
            src_ref=gall.at[lev, part],
            dst_ref=gall.at[lev, part],
            send_sem=sa.at[c * nl + i],
            recv_sem=ra.at[c * nl + i],
            device_id=(band, lax.rem(lev + i, nl)),
            device_id_type=MESH,
        )

    width = leg_ref.shape[2]
    used = 2 * lev_dev
    tail = 2 * used - BLK
    spare = used + 4
    order = iota((lat, width), 1)
    lane = iota((lat, BLK), 1)
    blank = jnp.zeros((lat, BLK - used - 4), F32)

    def transform(s):
        m = m_ref[band * S + s]
        keep = jnp.where(order >= m, 1.0, 0.0).astype(BF)
        coef = buf[s].reshape(used + 4, width)
        four = lax.dot_general(
            leg[s] * keep, coef, (((1,), (1,)), ((), ())), preferred_element_type=F32
        )
        return jnp.concatenate([four, blank], axis=1)

    def place(block, q, value):
        rows[block, pl.ds(q, lat, stride=Q), :] = value

    load_m.wait()
    load_surf.wait()
    load_again.wait()
    ends = [None] * Q
    for c, (start, count) in enumerate(CHUNKS):
        load_leg(c).wait()
        load_temp(c).wait()
        for q in range(Q):
            one = transform(start + q)
            place(start // Q, q, one)
            if count == 2 * Q:
                two = transform(start + Q + q)
                place(start // Q + 1, q, two)
                place(BLOCKS + c, q, jnp.where(lane < used, one, pltpu.roll(two, used, 1)))
                end = pltpu.roll(two, spare + c * tail - used + tail, 1)
                ends[q] = end if c == 0 else jnp.where(lane < spare + c * tail, ends[q], end)
            else:
                place(BLOCKS + c, q, jnp.where(lane < used, one, ends[q]))
        gall[lev, c * Q * lat : (c + 1) * Q * lat, :] = rows[BLOCKS + c].astype(BF)
        if c == 0:
            pl.semaphore_wait(barrier, nl - 1 + nb - 1)
        for i in range(1, nl):
            copy_a(i, c).start()
    for k in range(BLOCKS):
        full[lev, k * Q * lat : (k + 1) * Q * lat, :] = rows[k].astype(BF)

    depth = nl * BLK
    lev_total = h_ref.shape[1]
    load_h.wait()
    load_c.wait()
    row = iota((lev_dev, lev_total), 0) + lev * lev_dev
    col = iota((lev_dev, lev_total), 1)
    upper = jnp.where(col >= row, h[...].astype(F32), 0.0).astype(BF)
    row = iota((depth, lev_total), 0)
    col = iota((depth, lev_total), 1)
    spots = jnp.zeros((depth, lev_total), F32)
    for v in range(nl):
        step = row - v * BLK - 2 * (col - v * lev_dev)
        inside = (col >= v * lev_dev) & (col < (v + 1) * lev_dev)
        spots = jnp.where(inside & (step >= 0) & (step < 2), 1.0, spots)
    tall = lax.dot_general(
        spots.astype(BF), upper, (((1,), (1,)), ((), ())), preferred_element_type=F32
    )
    row = iota((depth, lev_dev), 0)
    mine = lev * BLK + 2 * lev_dev
    high = coup[...].astype(BF).astype(F32)
    tall = jnp.where(
        (row == mine) | (row == mine + 1), jnp.broadcast_to(high, (depth, lev_dev)), tall
    )
    tall = jnp.where(
        (row == mine + 2) | (row == mine + 3),
        jnp.broadcast_to(coup[...] - high, (depth, lev_dev)),
        tall,
    )
    tall = tall.astype(BF)
    row = iota((lev_dev, 2 * BLK), 0)
    col = iota((lev_dev, 2 * BLK), 1)
    odd = iota((depth, 2 * BLK), 0) & 1
    right = (iota((depth, 2 * BLK), 1) >= BLK).astype(jnp.int32)
    for t in range(3):
        onto = jnp.where((col & (BLK - 1)) == row + t * KP, 1.0, 0.0).astype(BF)
        spread_out = jnp.dot(tall, onto, preferred_element_type=F32)
        wide[t] = jnp.where(odd == right, spread_out, 0.0).astype(BF)

    build(1)

    for c in range(len(CHUNKS)):
        for i in range(1, nl):
            copy_a(i, c).wait()
    size = Q * lat
    lane = iota((size, BLK), 1)
    for i in range(1, nl):
        v = lax.rem(lev + i, nl)
        last = gall[v, 2 * size : 3 * size, :]
        full[v, 4 * size : 5 * size, :] = last
        last = last.astype(F32)
        for c in range(2):
            pair = gall[v, c * size : (c + 1) * size, :]
            full[v, 2 * c * size : (2 * c + 1) * size, :] = pair
            end = pltpu.roll(last, 2 * BLK + used - tail - spare - c * tail - BLK, 1)
            pair = jnp.where(lane < used - tail, pltpu.roll(pair.astype(F32), BLK - used, 1), end)
            full[v, (2 * c + 1) * size : (2 * c + 2) * size, :] = pair.astype(BF)

    group = 16
    pairs = group // 2

    def hydro(g):
        parts = []
        for k in range(BLOCKS):
            at = k * Q * lat + g * Q * group
            at = at if isinstance(at, int) else pl.multiple_of(at, 16)
            parts.append(pl.ds(at, Q * group))
        left = jnp.concatenate(
            [jnp.concatenate([full[v, p] for v in range(nl)], axis=1) for p in parts], axis=0
        )
        result = []
        for t in range(3):
            value = jnp.dot(left, wide[t], preferred_element_type=F32)
            value = value.reshape(BLOCKS, pairs, 2 * Q, 2 * BLK)
            result.append([value[:, p].reshape(PR, 2 * BLK) for p in range(pairs)])
        return result

    def pack(b, value):
        value = jnp.concatenate([value[:, :BLK], value[:, BLK:]], axis=0)
        pieces[b] = value.astype(BF)

    if lat == group:
        result = hydro(0)
        for b in range(nb):
            value = result[1][b]
            for t in (0, 2):
                if 0 <= b - 1 + t < pairs:
                    value = value + result[t][b - 1 + t]
            pack(b, value)
    else:
        total[...] = jnp.zeros_like(total)

        def many(g, _):
            result = hydro(g)
            for t in range(3):
                for p in range(pairs):
                    place = g * pairs + p + 2 - t
                    total[place] = total[place] + result[t][p]
            return 0

        def finish(b, _):
            pack(b, total[b + 1])
            return 0

        lax.fori_loop(0, lat // group, many, 0)
        lax.fori_loop(0, nb, finish, 0)

    def copy_b(i):
        peer = lax.rem(band + i, nb)
        return pltpu.make_async_remote_copy(
            src_ref=pieces.at[peer],
            dst_ref=out_ref.at[band],
            send_sem=sb.at[i],
            recv_sem=rb.at[i],
            device_id=(peer, lev),
            device_id_type=MESH,
        )

    def send(i, _):
        copy_b(i).start()
        return 0

    lax.fori_loop(1, nb, send, 0)
    out_ref[band] = pieces[band]
    half, near, far = halves(band, nb)

    def arrived(peer):
        copy_b(lax.rem(band - peer + nb, nb)).wait_recv()

    if early:
        build_table(m_ref, table, signs, nb)
        for k in range(2):
            sign[k] = signs[k * half * PR : (k + 1) * half * PR, :].T[:8]
    build(2)
    for k in range(1, half):
        arrived(near + lax.rem(band - near + k, half))
    if early:
        left = assemble(out_ref[pl.ds(near, half)], sign[band // half][:1])
        group = 4

        def synth(c, _):
            cols = pl.multiple_of(c * (group * BLK), 128)
            value = jnp.dot(
                left,
                table_part(table, near, half, pl.ds(cols, group * BLK)),
                preferred_element_type=F32,
            )
            partial[:, pl.ds(cols, group * BLK)] = value[: 2 * BLK]
            partial[:, pl.ds(cols + HALF_LON, group * BLK)] = value[2 * BLK :]
            return 0

        lax.fori_loop(0, XH // group, synth, 0, unroll=XH // group)
    build(3)

    def done(k, _):
        arrived(far + k)
        return 0

    def sent(i, _):
        copy_b(i).wait_send()
        return 0

    lax.fori_loop(0, half, done, 0)
    lax.fori_loop(1, nb, sent, 0)


def exchange(temp, surf, legendre, m_order, hydro, coupling, idx, wgt, nb, nl, early):
    _, lev_dev, _, width = temp.shape
    lat = legendre.shape[1]
    blocks = idx.shape[0]
    vmem = pl.BlockSpec(memory_space=pltpu.VMEM)
    hbm = pl.BlockSpec(memory_space=pltpu.HBM)
    out_shape = [
        jax.ShapeDtypeStruct((nb, 2 * PR, BLK), BF),
        jax.ShapeDtypeStruct((blocks, 2 * HALF, BLK), BF),
    ]
    if early:
        out_shape.append(jax.ShapeDtypeStruct((nb * PR, HALF_LON), BF))
        out_shape.append(jax.ShapeDtypeStruct((2 * BLK, NLON), F32))
        out_shape.append(jax.ShapeDtypeStruct((2, 8, nb // 2 * PR), F32))
    return pl.pallas_call(
        functools.partial(exchange_kernel, nb, nl, lat, lev_dev, early),
        out_shape=out_shape,
        in_specs=[hbm] * 8,
        out_specs=[vmem] * len(out_shape),
        scratch_shapes=[
            pltpu.VMEM((S, lev_dev + 2, 2, width), BF),
            pltpu.VMEM(legendre.shape, BF),
            pltpu.VMEM(hydro.shape, BF),
            pltpu.VMEM(coupling.shape, F32),
            pltpu.VMEM(idx.shape, jnp.int32),
            pltpu.VMEM(wgt.shape, F32),
            pltpu.SMEM(m_order.shape, jnp.int32),
            pltpu.VMEM((BLOCKS + len(CHUNKS), Q * lat, BLK), F32),
            pltpu.VMEM((nl, len(CHUNKS) * Q * lat, BLK), BF),
            pltpu.VMEM((nl, S * lat, BLK), BF),
            pltpu.VMEM((3, nl * BLK, 2 * BLK), BF),
            pltpu.VMEM((nb + 2 if lat > 16 else 1, PR, 2 * BLK), F32),
            pltpu.VMEM((nb, 2 * PR, BLK), BF),
            pltpu.VMEM((nb * PR, BLK), F32),
            pltpu.SemaphoreType.DMA((2 * len(CHUNKS),)),
            pltpu.SemaphoreType.DMA((7,)),
            pltpu.SemaphoreType.DMA((len(CHUNKS) * nl,)),
            pltpu.SemaphoreType.DMA((len(CHUNKS) * nl,)),
            pltpu.SemaphoreType.DMA((nb,)),
            pltpu.SemaphoreType.DMA((nb,)),
        ],
        compiler_params=pltpu.CompilerParams(
            collective_id=0, has_side_effects=True, vmem_limit_bytes=(30 if early else 52) * 1024 * 1024
        ),
    )(*[
        pltpu.with_memory_space_constraint(x, pltpu.HBM)
        for x in (temp, surf, legendre, m_order, hydro, coupling, idx, wgt)
    ])


def grid_kernel(nb, lev_dev, early, src_ref, coef_ref, spread, *refs):
    if early:
        table, partial, sign, out_ref, src, pool, grid, ss, so = refs
    else:
        m_ref, out_ref, src, pool, grid, ss, so, table, signs = refs
        build_table(m_ref, table, signs, nb)
    load_src = pltpu.make_async_copy(src_ref, src, ss)
    load_src.start()
    band = lax.axis_index("band")
    half, _, far = halves(band, nb)
    if early:
        left = assemble(coef_ref[pl.ds(far, half)], sign[far // half][:1])
    else:
        left = assemble(coef_ref[...], signs[...].T[:1])
    group = 4

    def synth(c, _):
        cols = pl.multiple_of(c * (group * BLK), 128)
        part = pl.ds(cols, group * BLK)
        part = table_part(table, far, half, part) if early else table[:, part]
        both = jnp.dot(left, part, preferred_element_type=F32)
        for side in range(2):
            value = both[side * 2 * BLK : (side + 1) * 2 * BLK]
            if early:
                value = value + partial[:, pl.ds(cols + side * HALF_LON, group * BLK)]
            value = value.astype(BF)
            for t in range(3):
                for p in range(2):
                    at = p * BLK + t * KP
                    for g in range(group):
                        pool[(2 * t + p) * XB + side * XH + c * group + g] = value[
                            at : at + KP, g * BLK : (g + 1) * BLK
                        ]
        return 0

    lax.fori_loop(0, XH // group, synth, 0, unroll=XH // group if early else 1)
    load_src.wait()

    first = (band - 1) * (2 * XB)

    def read(b):
        source = jnp.concatenate([pool[src[i, b] - first] for i in range(4)], axis=1)
        return jnp.dot(source, spread[b], preferred_element_type=F32)

    def write(q):
        cols = pl.ds(q * (STEP * BLK), STEP * BLK)
        return pltpu.make_async_copy(grid.at[:, :, cols], out_ref.at[:, :, cols], so.at[q])

    for q in range(XB // STEP):
        for x in range(q * STEP, (q + 1) * STEP):
            for j in range(2):
                grid[:, j, x * BLK : (x + 1) * BLK] = read(j * XB + x)[:lev_dev]
        write(q).start()
    for q in range(XB // STEP):
        write(q).wait()


def grid_part(src, m_order, coef, spread, table, nb, lev_dev):
    vmem = pl.BlockSpec(memory_space=pltpu.VMEM)
    hbm = pl.BlockSpec(memory_space=pltpu.HBM)
    early = len(table) > 0
    scratch = [
        pltpu.SMEM(src.shape, jnp.int32),
        pltpu.VMEM((JJ * XB, KP, BLK), BF),
        pltpu.VMEM((lev_dev, 2, NLON), F32),
        pltpu.SemaphoreType.DMA,
        pltpu.SemaphoreType.DMA((XB // STEP,)),
    ]
    src = pltpu.with_memory_space_constraint(src, pltpu.HBM)
    if early:
        last, specs = list(table), [vmem] * len(table)
    else:
        last, specs = [m_order], [pl.BlockSpec(memory_space=pltpu.SMEM)]
        scratch.append(pltpu.VMEM((nb * PR, HALF_LON), BF))
        scratch.append(pltpu.VMEM((nb * PR, BLK), F32))
    return pl.pallas_call(
        functools.partial(grid_kernel, nb, lev_dev, early),
        out_shape=jax.ShapeDtypeStruct((lev_dev, 2, NLON), F32),
        in_specs=[hbm, vmem, vmem] + specs,
        out_specs=hbm,
        scratch_shapes=scratch,
        compiler_params=pltpu.CompilerParams(
            vmem_limit_bytes=(24 if early else 54) * 1024 * 1024
        ),
    )(src, coef, spread, *last)


def shards(
    temp_spectrum,
    surf_spectrum,
    legendre,
    m_order,
    hydro_matrix,
    surf_coupling,
    src_blocks,
    tap_index,
    tap_weight,
):
    lev_dev = temp_spectrum.shape[3]
    nb, nl = lax.axis_size("band"), lax.axis_size("lev")
    early = nb <= 16
    coef, spread, *table = exchange(
        jnp.transpose(temp_spectrum, (0, 3, 2, 1)),
        jnp.transpose(surf_spectrum, (0, 2, 1)),
        legendre,
        m_order,
        hydro_matrix,
        surf_coupling[None, :],
        tap_index,
        tap_weight,
        nb,
        nl,
        early,
    )
    out = grid_part(src_blocks.T, m_order, coef, spread, table, nb, lev_dev)
    return jnp.transpose(out, (1, 0, 2))


def solution(mesh):
    in_specs = (
        P("band", None, None, "lev"),
        P("band", None, None),
        P("band", None, None),
        P(),
        P("lev", None),
        P("lev"),
        P("band", None),
        P("band", None, None),
        P("band", None, None),
    )
    out_specs = P("band", "lev", None)
    return jax.shard_map(shards, mesh=mesh, in_specs=in_specs, out_specs=out_specs, check_vma=False)
```

```python
import functools
import math

import jax
import jax.numpy as jnp
from jax import lax
from jax.experimental import pallas as pl
from jax.experimental.pallas import tpu as pltpu
from jax.sharding import PartitionSpec as P

NLON = 5120
BLK = 128
TAPS = 4
XB = NLON // BLK
XH = XB // 2
HALF_LON = NLON // 2
S = 20
CHUNKS = ((0, 8), (8, 8), (16, 4))
Q = 4
BLOCKS = S // Q
KP = 40
PR = 40
JJ = 6
HALF = 256
WORK = (5, 20, 15, 0)
KS = 48
STEP = 10
MESH = pl.DeviceIdType.MESH
BF = jnp.bfloat16
F32 = jnp.float32


def iota(shape, dim):
    return lax.broadcasted_iota(jnp.int32, shape, dim)


def cosine(steps):
    steps = steps - NLON * jnp.floor(steps * (1.0 / NLON))
    y = (jnp.abs(steps * (1.0 / NLON) - 0.5) - 0.25) * (2.0 * math.pi)
    z = y * y
    p = -1.0 / 39916800.0
    for c in (1.0 / 362880.0, -1.0 / 5040.0, 1.0 / 120.0, -1.0 / 6.0, 1.0):
        p = p * z + c
    return y * p


def table_rows(m_ref, table, signs, pair):
    row = iota((8, BLK), 0)
    point = iota((8, BLK), 1).astype(F32)
    first, second, turns, parity = [], [], [], []
    for u in range(2):
        base = (pair * 2 + u) * S
        orders = []
        for start, count in CHUNKS:
            tile = jnp.zeros((8, BLK), F32)
            for i in range(8):
                value = m_ref[base + start + i % count].astype(F32)
                tile = jnp.where(row == i, value, tile)
            orders.append(tile)
        turn = [2.0 * cosine(o * float(BLK)) for o in orders]
        shift = jnp.where(row >= 4, NLON // 4, 0).astype(F32)
        for c, s in ((0, 0.0), (1, 0.0), (0, NLON / 4), (1, NLON / 4), (2, shift)):
            factor = jnp.where(orders[c] == 0.0, 1.0, 2.0)
            first.append(factor * cosine(orders[c] * point + s))
            second.append(factor * cosine(orders[c] * (point + float(BLK)) + s))
            turns.append(turn[c])
            half = orders[c] * 0.5
            parity.append(1.0 - 4.0 * (half - jnp.floor(half)))
    old = jnp.concatenate(first, axis=0)
    new = jnp.concatenate(second, axis=0)
    turn = jnp.concatenate(turns, axis=0)
    place = pl.ds(pl.multiple_of(pair * 2 * PR, 16), 2 * PR)
    signs[place, :] = jnp.concatenate(parity, axis=0)
    for x in range(XH):
        table[place, x * BLK : (x + 1) * BLK] = old.astype(BF)
        old, new = new, turn * new - old


def build_table(m_ref, table, signs, nb):
    def pair(b, _):
        table_rows(m_ref, table, signs, b)
        return 0

    lax.fori_loop(0, nb // 2, pair, 0)


def build_spread(idx, wgt, spread, first, last):
    cells = iota((HALF, BLK), 0).astype(BF)
    zero = jnp.zeros((HALF, BLK), BF)

    def block(x, _):
        for j in range(2):
            index = idx[j * XB + x]
            weight = wgt[j * XB + x].astype(BF)
            for h in range(2):
                spot = (index - h * HALF).astype(F32).astype(BF)
                total = None
                for t in range(TAPS):
                    hit = cells == jnp.broadcast_to(spot[t : t + 1, :], (HALF, BLK))
                    part = jnp.where(
                        hit, jnp.broadcast_to(weight[t : t + 1, :], (HALF, BLK)), zero
                    )
                    total = part if total is None else total + part
                spread[x, h * HALF : (h + 1) * HALF, j * BLK : (j + 1) * BLK] = total
        return 0

    lax.fori_loop(first, last, block, 0)


def assemble(coef, sign):
    left = []
    for p in range(2):
        tiles = []
        for b in range(coef.shape[0]):
            value = coef[b].astype(F32)
            for r, k in [(r, k) for r in range(2) for k in range(4)] + [(0, 4), (1, 4)]:
                at = r * PR + k * 2 * Q + p * Q
                tiles.append(value[at : at + Q])
        left.append(jnp.concatenate(tiles, axis=0).T)
    left = jnp.concatenate(left, axis=0)
    return jnp.concatenate([left, left * sign], axis=0).astype(BF)


def halves(band, nb):
    half = nb // 2
    near = (band // half) * half
    return half, near, lax.rem(near + half, nb)


def table_part(table, start, half, cols):
    return table[pl.ds(pl.multiple_of(start * PR, 16), half * PR), cols]


def exchange_kernel(
    nb, nl, lat, lev_dev, early, *refs
):
    (temp_ref, surf_ref, leg_ref, ord_ref, h_ref, c_ref, idx_ref, wgt_ref), refs = refs[:8], refs[8:]
    out_ref, spread = refs[:2]
    if early:
        table, partial, sign = refs[2:5]
    refs = refs[2 + 3 * early :]
    (buf, leg, h, coup, idx, wgt, m_ref, rows, gall, full, wide, total, pieces, signs) = refs[:14]
    (sl, sm, sa, ra, sb, rb) = refs[14:]
    band = lax.axis_index("band")
    lev = lax.axis_index("lev")
    chunks = len(CHUNKS)

    def load_temp(c):
        part = pl.ds(*CHUNKS[c])
        return pltpu.make_async_copy(temp_ref.at[part], buf.at[part, pl.ds(0, lev_dev)], sl.at[c])

    def load_leg(c):
        part = pl.ds(*CHUNKS[c])
        return pltpu.make_async_copy(leg_ref.at[part], leg.at[part], sl.at[chunks + c])

    load_surf = pltpu.make_async_copy(surf_ref, buf.at[:, lev_dev], sm.at[0])
    load_again = pltpu.make_async_copy(surf_ref, buf.at[:, lev_dev + 1], sm.at[6])
    load_h = pltpu.make_async_copy(h_ref, h, sm.at[1])
    load_c = pltpu.make_async_copy(c_ref, coup, sm.at[2])
    load_idx = pltpu.make_async_copy(idx_ref, idx, sm.at[3])
    load_wgt = pltpu.make_async_copy(wgt_ref, wgt, sm.at[4])
    load_m = pltpu.make_async_copy(ord_ref, m_ref, sm.at[5])
    load_idx.start()
    load_wgt.start()
    load_m.start()
    load_surf.start()
    load_again.start()
    load_leg(0).start()
    load_temp(0).start()

    barrier = pltpu.get_barrier_semaphore()

    def greet_lev(i, _):
        pl.semaphore_signal(
            barrier, inc=1, device_id=(band, lax.rem(lev + i, nl)), device_id_type=MESH
        )
        return 0

    def greet_band(i, _):
        pl.semaphore_signal(
            barrier, inc=1, device_id=(lax.rem(band + i, nb), lev), device_id_type=MESH
        )
        return 0

    lax.fori_loop(1, nb, greet_band, 0)
    lax.fori_loop(1, nl, greet_lev, 0)
    for c in range(1, chunks):
        load_leg(c).start()
        load_temp(c).start()
    load_h.start()
    load_c.start()
    load_idx.wait()
    load_wgt.wait()
    marks = [0]
    for count in WORK:
        marks.append(marks[-1] + count)
    assert 2 * marks[-1] == idx.shape[0]

    def build(part):
        build_spread(idx, wgt, spread, marks[part], marks[part + 1])

    build(0)

    def copy_a(i, c):
        part = pl.ds(c * Q * lat, Q * lat)
        return pltpu.make_async_remote_copy(
            src_ref=gall.at[lev, part],
            dst_ref=gall.at[lev, part],
            send_sem=sa.at[c * nl + i],
            recv_sem=ra.at[c * nl + i],
            device_id=(band, lax.rem(lev + i, nl)),
            device_id_type=MESH,
        )

    width = leg_ref.shape[2]
    used = 2 * lev_dev
    tail = 2 * used - BLK
    spare = used + 4
    order = iota((lat, width), 1)
    lane = iota((lat, BLK), 1)
    blank = jnp.zeros((lat, BLK - used - 4), F32)

    def transform(s):
        m = m_ref[band * S + s]
        keep = jnp.where(order >= m, 1.0, 0.0).astype(BF)
        coef = buf[s].reshape(used + 4, width)
        four = lax.dot_general(
            leg[s] * keep, coef, (((1,), (1,)), ((), ())), preferred_element_type=F32
        )
        return jnp.concatenate([four, blank], axis=1)

    def place(block, q, value):
        rows[block, pl.ds(q, lat, stride=Q), :] = value

    load_m.wait()
    load_surf.wait()
    load_again.wait()
    ends = [None] * Q
    for c, (start, count) in enumerate(CHUNKS):
        load_leg(c).wait()
        load_temp(c).wait()
        for q in range(Q):
            one = transform(start + q)
            place(start // Q, q, one)
            if count == 2 * Q:
                two = transform(start + Q + q)
                place(start // Q + 1, q, two)
                place(BLOCKS + c, q, jnp.where(lane < used, one, pltpu.roll(two, used, 1)))
                end = pltpu.roll(two, spare + c * tail - used + tail, 1)
                ends[q] = end if c == 0 else jnp.where(lane < spare + c * tail, ends[q], end)
            else:
                place(BLOCKS + c, q, jnp.where(lane < used, one, ends[q]))
        gall[lev, c * Q * lat : (c + 1) * Q * lat, :] = rows[BLOCKS + c].astype(BF)
        if c == 0:
            pl.semaphore_wait(barrier, nl - 1 + nb - 1)
        for i in range(1, nl):
            copy_a(i, c).start()
    for k in range(BLOCKS):
        full[lev, k * Q * lat : (k + 1) * Q * lat, :] = rows[k].astype(BF)

    depth = nl * BLK
    lev_total = h_ref.shape[1]
    load_h.wait()
    load_c.wait()
    row = iota((lev_dev, lev_total), 0) + lev * lev_dev
    col = iota((lev_dev, lev_total), 1)
    upper = jnp.where(col >= row, h[...].astype(F32), 0.0).astype(BF)
    row = iota((depth, lev_total), 0)
    col = iota((depth, lev_total), 1)
    spots = jnp.zeros((depth, lev_total), F32)
    for v in range(nl):
        step = row - v * BLK - 2 * (col - v * lev_dev)
        inside = (col >= v * lev_dev) & (col < (v + 1) * lev_dev)
        spots = jnp.where(inside & (step >= 0) & (step < 2), 1.0, spots)
    tall = lax.dot_general(
        spots.astype(BF), upper, (((1,), (1,)), ((), ())), preferred_element_type=F32
    )
    row = iota((depth, lev_dev), 0)
    mine = lev * BLK + 2 * lev_dev
    high = coup[...].astype(BF).astype(F32)
    tall = jnp.where(
        (row == mine) | (row == mine + 1), jnp.broadcast_to(high, (depth, lev_dev)), tall
    )
    tall = jnp.where(
        (row == mine + 2) | (row == mine + 3),
        jnp.broadcast_to(coup[...] - high, (depth, lev_dev)),
        tall,
    )
    tall = tall.astype(BF)
    row = iota((lev_dev, 2 * BLK), 0)
    col = iota((lev_dev, 2 * BLK), 1)
    odd = iota((depth, 2 * BLK), 0) & 1
    right = (iota((depth, 2 * BLK), 1) >= BLK).astype(jnp.int32)
    for t in range(3):
        onto = jnp.where((col & (BLK - 1)) == row + t * KP, 1.0, 0.0).astype(BF)
        spread_out = jnp.dot(tall, onto, preferred_element_type=F32)
        wide[t] = jnp.where(odd == right, spread_out, 0.0).astype(BF)

    build(1)

    for c in range(len(CHUNKS)):
        for i in range(1, nl):
            copy_a(i, c).wait()
    size = Q * lat
    lane = iota((size, BLK), 1)
    for i in range(1, nl):
        v = lax.rem(lev + i, nl)
        last = gall[v, 2 * size : 3 * size, :]
        full[v, 4 * size : 5 * size, :] = last
        last = last.astype(F32)
        for c in range(2):
            pair = gall[v, c * size : (c + 1) * size, :]
            full[v, 2 * c * size : (2 * c + 1) * size, :] = pair
            end = pltpu.roll(last, 2 * BLK + used - tail - spare - c * tail - BLK, 1)
            pair = jnp.where(lane < used - tail, pltpu.roll(pair.astype(F32), BLK - used, 1), end)
            full[v, (2 * c + 1) * size : (2 * c + 2) * size, :] = pair.astype(BF)

    group = 16
    pairs = group // 2

    def hydro(g):
        parts = []
        for k in range(BLOCKS):
            at = k * Q * lat + g * Q * group
            at = at if isinstance(at, int) else pl.multiple_of(at, 16)
            parts.append(pl.ds(at, Q * group))
        left = jnp.concatenate(
            [jnp.concatenate([full[v, p] for v in range(nl)], axis=1) for p in parts], axis=0
        )
        result = []
        for t in range(3):
            value = jnp.dot(left, wide[t], preferred_element_type=F32)
            value = value.reshape(BLOCKS, pairs, 2 * Q, 2 * BLK)
            result.append([value[:, p].reshape(PR, 2 * BLK) for p in range(pairs)])
        return result

    def pack(b, value):
        value = jnp.concatenate([value[:, :BLK], value[:, BLK:]], axis=0)
        pieces[b] = value.astype(BF)

    if lat == group:
        result = hydro(0)
        for b in range(nb):
            value = result[1][b]
            for t in (0, 2):
                if 0 <= b - 1 + t < pairs:
                    value = value + result[t][b - 1 + t]
            pack(b, value)
    else:
        total[...] = jnp.zeros_like(total)

        def many(g, _):
            result = hydro(g)
            for t in range(3):
                for p in range(pairs):
                    place = g * pairs + p + 2 - t
                    total[place] = total[place] + result[t][p]
            return 0

        def finish(b, _):
            pack(b, total[b + 1])
            return 0

        lax.fori_loop(0, lat // group, many, 0)
        lax.fori_loop(0, nb, finish, 0)

    def copy_b(i):
        peer = lax.rem(band + i, nb)
        return pltpu.make_async_remote_copy(
            src_ref=pieces.at[peer],
            dst_ref=out_ref.at[band],
            send_sem=sb.at[i],
            recv_sem=rb.at[i],
            device_id=(peer, lev),
            device_id_type=MESH,
        )

    def send(i, _):
        copy_b(i).start()
        return 0

    lax.fori_loop(1, nb, send, 0)
    out_ref[band] = pieces[band]
    half, near, far = halves(band, nb)

    def arrived(peer):
        copy_b(lax.rem(band - peer + nb, nb)).wait_recv()

    if early:
        build_table(m_ref, table, signs, nb)
        for k in range(2):
            sign[k] = signs[k * half * PR : (k + 1) * half * PR, :].T[:8]
    build(2)
    for k in range(1, half):
        arrived(near + lax.rem(band - near + k, half))
    if early:
        left = assemble(out_ref[pl.ds(near, half)], sign[band // half][:1])
        group = 4

        def synth(c, _):
            cols = pl.multiple_of(c * (group * BLK), 128)
            value = jnp.dot(
                left,
                table_part(table, near, half, pl.ds(cols, group * BLK)),
                preferred_element_type=F32,
            )
            partial[:, pl.ds(cols, group * BLK)] = value[: 2 * BLK]
            partial[:, pl.ds(cols + HALF_LON, group * BLK)] = value[2 * BLK :]
            return 0

        lax.fori_loop(0, XH // group, synth, 0, unroll=XH // group)
    build(3)

    def done(k, _):
        arrived(far + k)
        return 0

    def sent(i, _):
        copy_b(i).wait_send()
        return 0

    lax.fori_loop(0, half, done, 0)
    lax.fori_loop(1, nb, sent, 0)


def exchange(temp, surf, legendre, m_order, hydro, coupling, idx, wgt, nb, nl, early):
    _, lev_dev, _, width = temp.shape
    lat = legendre.shape[1]
    blocks = idx.shape[0]
    vmem = pl.BlockSpec(memory_space=pltpu.VMEM)
    hbm = pl.BlockSpec(memory_space=pltpu.HBM)
    out_shape = [
        jax.ShapeDtypeStruct((nb, 2 * PR, BLK), BF),
        jax.ShapeDtypeStruct((blocks // 2, 2 * HALF, 2 * BLK), BF),
    ]
    if early:
        out_shape.append(jax.ShapeDtypeStruct((nb * PR, HALF_LON), BF))
        out_shape.append(jax.ShapeDtypeStruct((2 * BLK, NLON), F32))
        out_shape.append(jax.ShapeDtypeStruct((2, 8, nb // 2 * PR), F32))
    return pl.pallas_call(
        functools.partial(exchange_kernel, nb, nl, lat, lev_dev, early),
        out_shape=out_shape,
        in_specs=[hbm] * 8,
        out_specs=[vmem] * len(out_shape),
        scratch_shapes=[
            pltpu.VMEM((S, lev_dev + 2, 2, width), BF),
            pltpu.VMEM(legendre.shape, BF),
            pltpu.VMEM(hydro.shape, BF),
            pltpu.VMEM(coupling.shape, F32),
            pltpu.VMEM(idx.shape, jnp.int32),
            pltpu.VMEM(wgt.shape, F32),
            pltpu.SMEM(m_order.shape, jnp.int32),
            pltpu.VMEM((BLOCKS + len(CHUNKS), Q * lat, BLK), F32),
            pltpu.VMEM((nl, len(CHUNKS) * Q * lat, BLK), BF),
            pltpu.VMEM((nl, S * lat, BLK), BF),
            pltpu.VMEM((3, nl * BLK, 2 * BLK), BF),
            pltpu.VMEM((nb + 2 if lat > 16 else 1, PR, 2 * BLK), F32),
            pltpu.VMEM((nb, 2 * PR, BLK), BF),
            pltpu.VMEM((nb * PR, BLK), F32),
            pltpu.SemaphoreType.DMA((2 * len(CHUNKS),)),
            pltpu.SemaphoreType.DMA((7,)),
            pltpu.SemaphoreType.DMA((len(CHUNKS) * nl,)),
            pltpu.SemaphoreType.DMA((len(CHUNKS) * nl,)),
            pltpu.SemaphoreType.DMA((nb,)),
            pltpu.SemaphoreType.DMA((nb,)),
        ],
        compiler_params=pltpu.CompilerParams(
            collective_id=0, has_side_effects=True, vmem_limit_bytes=(30 if early else 52) * 1024 * 1024
        ),
    )(*[
        pltpu.with_memory_space_constraint(x, pltpu.HBM)
        for x in (temp, surf, legendre, m_order, hydro, coupling, idx, wgt)
    ])


def grid_kernel(nb, lev_dev, early, src_ref, coef_ref, spread, *refs):
    if early:
        table, partial, sign, out_ref, src, pool, grid, ss, so = refs
    else:
        m_ref, out_ref, src, pool, grid, ss, so, table, signs = refs
        build_table(m_ref, table, signs, nb)
    load_src = pltpu.make_async_copy(src_ref, src, ss)
    load_src.start()
    band = lax.axis_index("band")
    half, _, far = halves(band, nb)
    if early:
        left = assemble(coef_ref[pl.ds(far, half)], sign[far // half][:1])
    else:
        left = assemble(coef_ref[...], signs[...].T[:1])
    group = 4

    def synth(c, _):
        cols = pl.multiple_of(c * (group * BLK), 128)
        part = pl.ds(cols, group * BLK)
        part = table_part(table, far, half, part) if early else table[:, part]
        both = jnp.dot(left, part, preferred_element_type=F32)
        for side in range(2):
            value = both[side * 2 * BLK : (side + 1) * 2 * BLK]
            if early:
                value = value + partial[:, pl.ds(cols + side * HALF_LON, group * BLK)]
            value = value.astype(BF)
            for t in range(3):
                for p in range(2):
                    at = p * BLK + t * KP
                    for g in range(group):
                        pool[(2 * t + p) * XB + side * XH + c * group + g, :KP] = value[
                            at : at + KP, g * BLK : (g + 1) * BLK
                        ]
        return 0

    lax.fori_loop(0, XH // group, synth, 0, unroll=XH // group if early else 1)
    load_src.wait()

    first = (band - 1) * (2 * XB)

    def read(x):
        source = jnp.concatenate(
            [
                jnp.concatenate([pool[src[i, j * XB + x] - first] for i in range(4)], axis=1)
                for j in range(2)
            ],
            axis=0,
        )
        return jnp.dot(source, spread[x], preferred_element_type=F32)

    def write(q):
        cols = pl.ds(q * (STEP * BLK), STEP * BLK)
        return pltpu.make_async_copy(grid.at[:, :, cols], out_ref.at[:, :, cols], so.at[q])

    for q in range(XB // STEP):
        for x in range(q * STEP, (q + 1) * STEP):
            value = read(x)
            for j in range(2):
                grid[:, j, x * BLK : (x + 1) * BLK] = value[
                    j * KS : j * KS + lev_dev, j * BLK : (j + 1) * BLK
                ]
        write(q).start()
    for q in range(XB // STEP):
        write(q).wait()


def grid_part(src, m_order, coef, spread, table, nb, lev_dev):
    vmem = pl.BlockSpec(memory_space=pltpu.VMEM)
    hbm = pl.BlockSpec(memory_space=pltpu.HBM)
    early = len(table) > 0
    scratch = [
        pltpu.SMEM(src.shape, jnp.int32),
        pltpu.VMEM((JJ * XB, KS, BLK), BF),
        pltpu.VMEM((lev_dev, 2, NLON), F32),
        pltpu.SemaphoreType.DMA,
        pltpu.SemaphoreType.DMA((XB // STEP,)),
    ]
    src = pltpu.with_memory_space_constraint(src, pltpu.HBM)
    if early:
        last, specs = list(table), [vmem] * len(table)
    else:
        last, specs = [m_order], [pl.BlockSpec(memory_space=pltpu.SMEM)]
        scratch.append(pltpu.VMEM((nb * PR, HALF_LON), BF))
        scratch.append(pltpu.VMEM((nb * PR, BLK), F32))
    return pl.pallas_call(
        functools.partial(grid_kernel, nb, lev_dev, early),
        out_shape=jax.ShapeDtypeStruct((lev_dev, 2, NLON), F32),
        in_specs=[hbm, vmem, vmem] + specs,
        out_specs=hbm,
        scratch_shapes=scratch,
        compiler_params=pltpu.CompilerParams(
            vmem_limit_bytes=(24 if early else 54) * 1024 * 1024
        ),
    )(src, coef, spread, *last)


def shards(
    temp_spectrum,
    surf_spectrum,
    legendre,
    m_order,
    hydro_matrix,
    surf_coupling,
    src_blocks,
    tap_index,
    tap_weight,
):
    lev_dev = temp_spectrum.shape[3]
    nb, nl = lax.axis_size("band"), lax.axis_size("lev")
    early = nb <= 16
    coef, spread, *table = exchange(
        jnp.transpose(temp_spectrum, (0, 3, 2, 1)),
        jnp.transpose(surf_spectrum, (0, 2, 1)),
        legendre,
        m_order,
        hydro_matrix,
        surf_coupling[None, :],
        tap_index,
        tap_weight,
        nb,
        nl,
        early,
    )
    out = grid_part(src_blocks.T, m_order, coef, spread, table, nb, lev_dev)
    return jnp.transpose(out, (1, 0, 2))


def solution(mesh):
    in_specs = (
        P("band", None, None, "lev"),
        P("band", None, None),
        P("band", None, None),
        P(),
        P("lev", None),
        P("lev"),
        P("band", None),
        P("band", None, None),
        P("band", None, None),
    )
    out_specs = P("band", "lev", None)
    return jax.shard_map(shards, mesh=mesh, in_specs=in_specs, out_specs=out_specs, check_vma=False)
```

```python
import functools
import math

import jax
import jax.numpy as jnp
from jax import lax
from jax.experimental import pallas as pl
from jax.experimental.pallas import tpu as pltpu
from jax.sharding import PartitionSpec as P

NLON = 5120
BLK = 128
TAPS = 4
XB = NLON // BLK
XH = XB // 2
HALF_LON = NLON // 2
S = 20
CHUNKS = ((0, 8), (8, 8), (16, 4))
Q = 4
BLOCKS = S // Q
KP = 40
PR = 40
JJ = 6
HALF = 256
WORK = (5, 20, 15, 0)
KS = 48
PARTS = (14, 14, 8, 4)
MESH = pl.DeviceIdType.MESH
BF = jnp.bfloat16
F32 = jnp.float32


def iota(shape, dim):
    return lax.broadcasted_iota(jnp.int32, shape, dim)


def cosine(steps):
    steps = steps - NLON * jnp.floor(steps * (1.0 / NLON))
    y = (jnp.abs(steps * (1.0 / NLON) - 0.5) - 0.25) * (2.0 * math.pi)
    z = y * y
    p = -1.0 / 39916800.0
    for c in (1.0 / 362880.0, -1.0 / 5040.0, 1.0 / 120.0, -1.0 / 6.0, 1.0):
        p = p * z + c
    return y * p


def table_rows(m_ref, table, signs, pair):
    row = iota((8, BLK), 0)
    point = iota((8, BLK), 1).astype(F32)
    first, second, turns, parity = [], [], [], []
    for u in range(2):
        base = (pair * 2 + u) * S
        orders = []
        for start, count in CHUNKS:
            tile = jnp.zeros((8, BLK), F32)
            for i in range(8):
                value = m_ref[base + start + i % count].astype(F32)
                tile = jnp.where(row == i, value, tile)
            orders.append(tile)
        turn = [2.0 * cosine(o * float(BLK)) for o in orders]
        shift = jnp.where(row >= 4, NLON // 4, 0).astype(F32)
        for c, s in ((0, 0.0), (1, 0.0), (0, NLON / 4), (1, NLON / 4), (2, shift)):
            factor = jnp.where(orders[c] == 0.0, 1.0, 2.0)
            first.append(factor * cosine(orders[c] * point + s))
            second.append(factor * cosine(orders[c] * (point + float(BLK)) + s))
            turns.append(turn[c])
            half = orders[c] * 0.5
            parity.append(1.0 - 4.0 * (half - jnp.floor(half)))
    old = jnp.concatenate(first, axis=0)
    new = jnp.concatenate(second, axis=0)
    turn = jnp.concatenate(turns, axis=0)
    place = pl.ds(pl.multiple_of(pair * 2 * PR, 16), 2 * PR)
    signs[place, :] = jnp.concatenate(parity, axis=0)
    for x in range(XH):
        table[place, x * BLK : (x + 1) * BLK] = old.astype(BF)
        old, new = new, turn * new - old


def build_table(m_ref, table, signs, nb):
    def pair(b, _):
        table_rows(m_ref, table, signs, b)
        return 0

    lax.fori_loop(0, nb // 2, pair, 0)


def build_spread(idx, wgt, spread, first, last):
    cells = iota((HALF, BLK), 0).astype(BF)
    zero = jnp.zeros((HALF, BLK), BF)

    def block(x, _):
        for j in range(2):
            index = idx[j * XB + x]
            weight = wgt[j * XB + x].astype(BF)
            for h in range(2):
                spot = (index - h * HALF).astype(F32).astype(BF)
                total = None
                for t in range(TAPS):
                    hit = cells == jnp.broadcast_to(spot[t : t + 1, :], (HALF, BLK))
                    part = jnp.where(
                        hit, jnp.broadcast_to(weight[t : t + 1, :], (HALF, BLK)), zero
                    )
                    total = part if total is None else total + part
                spread[x, h * HALF : (h + 1) * HALF, j * BLK : (j + 1) * BLK] = total
        return 0

    lax.fori_loop(first, last, block, 0)


def assemble(coef, sign):
    left = []
    for p in range(2):
        tiles = []
        for b in range(coef.shape[0]):
            value = coef[b].astype(F32)
            for r, k in [(r, k) for r in range(2) for k in range(4)] + [(0, 4), (1, 4)]:
                at = r * PR + k * 2 * Q + p * Q
                tiles.append(value[at : at + Q])
        left.append(jnp.concatenate(tiles, axis=0).T)
    left = jnp.concatenate(left, axis=0)
    return jnp.concatenate([left, left * sign], axis=0).astype(BF)


def halves(band, nb):
    half = nb // 2
    near = (band // half) * half
    return half, near, lax.rem(near + half, nb)


def table_part(table, start, half, cols):
    return table[pl.ds(pl.multiple_of(start * PR, 16), half * PR), cols]


def exchange_kernel(
    nb, nl, lat, lev_dev, early, *refs
):
    (temp_ref, surf_ref, leg_ref, ord_ref, h_ref, c_ref, idx_ref, wgt_ref), refs = refs[:8], refs[8:]
    out_ref, spread = refs[:2]
    if early:
        table, partial, sign = refs[2:5]
    refs = refs[2 + 3 * early :]
    (buf, leg, h, coup, idx, wgt, m_ref, rows, gall, full, wide, total, pieces, signs) = refs[:14]
    (sl, sm, sa, ra, sb, rb) = refs[14:]
    band = lax.axis_index("band")
    lev = lax.axis_index("lev")
    chunks = len(CHUNKS)

    def load_temp(c):
        part = pl.ds(*CHUNKS[c])
        return pltpu.make_async_copy(temp_ref.at[part], buf.at[part, pl.ds(0, lev_dev)], sl.at[c])

    def load_leg(c):
        part = pl.ds(*CHUNKS[c])
        return pltpu.make_async_copy(leg_ref.at[part], leg.at[part], sl.at[chunks + c])

    load_surf = pltpu.make_async_copy(surf_ref, buf.at[:, lev_dev], sm.at[0])
    load_again = pltpu.make_async_copy(surf_ref, buf.at[:, lev_dev + 1], sm.at[6])
    load_h = pltpu.make_async_copy(h_ref, h, sm.at[1])
    load_c = pltpu.make_async_copy(c_ref, coup, sm.at[2])
    load_idx = pltpu.make_async_copy(idx_ref, idx, sm.at[3])
    load_wgt = pltpu.make_async_copy(wgt_ref, wgt, sm.at[4])
    load_m = pltpu.make_async_copy(ord_ref, m_ref, sm.at[5])
    load_idx.start()
    load_wgt.start()
    load_m.start()
    load_surf.start()
    load_again.start()
    load_leg(0).start()
    load_temp(0).start()

    barrier = pltpu.get_barrier_semaphore()

    def greet_lev(i, _):
        pl.semaphore_signal(
            barrier, inc=1, device_id=(band, lax.rem(lev + i, nl)), device_id_type=MESH
        )
        return 0

    def greet_band(i, _):
        pl.semaphore_signal(
            barrier, inc=1, device_id=(lax.rem(band + i, nb), lev), device_id_type=MESH
        )
        return 0

    lax.fori_loop(1, nb, greet_band, 0)
    lax.fori_loop(1, nl, greet_lev, 0)
    for c in range(1, chunks):
        load_leg(c).start()
        load_temp(c).start()
    load_h.start()
    load_c.start()
    load_idx.wait()
    load_wgt.wait()
    marks = [0]
    for count in WORK:
        marks.append(marks[-1] + count)
    assert 2 * marks[-1] == idx.shape[0]

    def build(part):
        build_spread(idx, wgt, spread, marks[part], marks[part + 1])

    build(0)

    def copy_a(i, c):
        part = pl.ds(c * Q * lat, Q * lat)
        return pltpu.make_async_remote_copy(
            src_ref=gall.at[lev, part],
            dst_ref=gall.at[lev, part],
            send_sem=sa.at[c * nl + i],
            recv_sem=ra.at[c * nl + i],
            device_id=(band, lax.rem(lev + i, nl)),
            device_id_type=MESH,
        )

    width = leg_ref.shape[2]
    used = 2 * lev_dev
    tail = 2 * used - BLK
    spare = used + 4
    order = iota((lat, width), 1)
    lane = iota((lat, BLK), 1)
    blank = jnp.zeros((lat, BLK - used - 4), F32)

    def transform(s):
        m = m_ref[band * S + s]
        keep = jnp.where(order >= m, 1.0, 0.0).astype(BF)
        coef = buf[s].reshape(used + 4, width)
        four = lax.dot_general(
            leg[s] * keep, coef, (((1,), (1,)), ((), ())), preferred_element_type=F32
        )
        return jnp.concatenate([four, blank], axis=1)

    def place(block, q, value):
        rows[block, pl.ds(q, lat, stride=Q), :] = value

    load_m.wait()
    load_surf.wait()
    load_again.wait()
    ends = [None] * Q
    for c, (start, count) in enumerate(CHUNKS):
        load_leg(c).wait()
        load_temp(c).wait()
        for q in range(Q):
            one = transform(start + q)
            place(start // Q, q, one)
            if count == 2 * Q:
                two = transform(start + Q + q)
                place(start // Q + 1, q, two)
                place(BLOCKS + c, q, jnp.where(lane < used, one, pltpu.roll(two, used, 1)))
                end = pltpu.roll(two, spare + c * tail - used + tail, 1)
                ends[q] = end if c == 0 else jnp.where(lane < spare + c * tail, ends[q], end)
            else:
                place(BLOCKS + c, q, jnp.where(lane < used, one, ends[q]))
        gall[lev, c * Q * lat : (c + 1) * Q * lat, :] = rows[BLOCKS + c].astype(BF)
        if c == 0:
            pl.semaphore_wait(barrier, nl - 1 + nb - 1)
        for i in range(1, nl):
            copy_a(i, c).start()
    for k in range(BLOCKS):
        full[lev, k * Q * lat : (k + 1) * Q * lat, :] = rows[k].astype(BF)

    depth = nl * BLK
    lev_total = h_ref.shape[1]
    load_h.wait()
    load_c.wait()
    row = iota((lev_dev, lev_total), 0) + lev * lev_dev
    col = iota((lev_dev, lev_total), 1)
    upper = jnp.where(col >= row, h[...].astype(F32), 0.0).astype(BF)
    row = iota((depth, lev_total), 0)
    col = iota((depth, lev_total), 1)
    spots = jnp.zeros((depth, lev_total), F32)
    for v in range(nl):
        step = row - v * BLK - 2 * (col - v * lev_dev)
        inside = (col >= v * lev_dev) & (col < (v + 1) * lev_dev)
        spots = jnp.where(inside & (step >= 0) & (step < 2), 1.0, spots)
    tall = lax.dot_general(
        spots.astype(BF), upper, (((1,), (1,)), ((), ())), preferred_element_type=F32
    )
    row = iota((depth, lev_dev), 0)
    mine = lev * BLK + 2 * lev_dev
    high = coup[...].astype(BF).astype(F32)
    tall = jnp.where(
        (row == mine) | (row == mine + 1), jnp.broadcast_to(high, (depth, lev_dev)), tall
    )
    tall = jnp.where(
        (row == mine + 2) | (row == mine + 3),
        jnp.broadcast_to(coup[...] - high, (depth, lev_dev)),
        tall,
    )
    tall = tall.astype(BF)
    row = iota((lev_dev, 2 * BLK), 0)
    col = iota((lev_dev, 2 * BLK), 1)
    odd = iota((depth, 2 * BLK), 0) & 1
    right = (iota((depth, 2 * BLK), 1) >= BLK).astype(jnp.int32)
    for t in range(3):
        onto = jnp.where((col & (BLK - 1)) == row + t * KP, 1.0, 0.0).astype(BF)
        spread_out = jnp.dot(tall, onto, preferred_element_type=F32)
        wide[t] = jnp.where(odd == right, spread_out, 0.0).astype(BF)

    build(1)

    for c in range(len(CHUNKS)):
        for i in range(1, nl):
            copy_a(i, c).wait()
    size = Q * lat
    lane = iota((size, BLK), 1)
    for i in range(1, nl):
        v = lax.rem(lev + i, nl)
        last = gall[v, 2 * size : 3 * size, :]
        full[v, 4 * size : 5 * size, :] = last
        last = last.astype(F32)
        for c in range(2):
            pair = gall[v, c * size : (c + 1) * size, :]
            full[v, 2 * c * size : (2 * c + 1) * size, :] = pair
            end = pltpu.roll(last, 2 * BLK + used - tail - spare - c * tail - BLK, 1)
            pair = jnp.where(lane < used - tail, pltpu.roll(pair.astype(F32), BLK - used, 1), end)
            full[v, (2 * c + 1) * size : (2 * c + 2) * size, :] = pair.astype(BF)

    group = 16
    pairs = group // 2

    def hydro(g):
        parts = []
        for k in range(BLOCKS):
            at = k * Q * lat + g * Q * group
            at = at if isinstance(at, int) else pl.multiple_of(at, 16)
            parts.append(pl.ds(at, Q * group))
        left = jnp.concatenate(
            [jnp.concatenate([full[v, p] for v in range(nl)], axis=1) for p in parts], axis=0
        )
        result = []
        for t in range(3):
            value = jnp.dot(left, wide[t], preferred_element_type=F32)
            value = value.reshape(BLOCKS, pairs, 2 * Q, 2 * BLK)
            result.append([value[:, p].reshape(PR, 2 * BLK) for p in range(pairs)])
        return result

    def pack(b, value):
        value = jnp.concatenate([value[:, :BLK], value[:, BLK:]], axis=0)
        pieces[b] = value.astype(BF)

    if lat == group:
        result = hydro(0)
        for b in range(nb):
            value = result[1][b]
            for t in (0, 2):
                if 0 <= b - 1 + t < pairs:
                    value = value + result[t][b - 1 + t]
            pack(b, value)
    else:
        total[...] = jnp.zeros_like(total)

        def many(g, _):
            result = hydro(g)
            for t in range(3):
                for p in range(pairs):
                    place = g * pairs + p + 2 - t
                    total[place] = total[place] + result[t][p]
            return 0

        def finish(b, _):
            pack(b, total[b + 1])
            return 0

        lax.fori_loop(0, lat // group, many, 0)
        lax.fori_loop(0, nb, finish, 0)

    def copy_b(i):
        peer = lax.rem(band + i, nb)
        return pltpu.make_async_remote_copy(
            src_ref=pieces.at[peer],
            dst_ref=out_ref.at[band],
            send_sem=sb.at[i],
            recv_sem=rb.at[i],
            device_id=(peer, lev),
            device_id_type=MESH,
        )

    half, near, far = halves(band, nb)

    def send(peer):
        copy_b(lax.rem(peer - band + nb, nb)).start()

    def send_far(k, _):
        send(far + jnp.where(far > 0, half - 1 - k, k))
        return 0

    def send_near(k, _):
        send(near + lax.rem(band - near + k, half))
        return 0

    lax.fori_loop(0, half, send_far, 0)
    lax.fori_loop(1, half, send_near, 0)
    out_ref[band] = pieces[band]
    def arrived(peer):
        copy_b(lax.rem(band - peer + nb, nb)).wait_recv()

    if early:
        build_table(m_ref, table, signs, nb)
        for k in range(2):
            sign[k] = signs[k * half * PR : (k + 1) * half * PR, :].T[:8]
    build(2)
    for k in range(1, half):
        arrived(near + lax.rem(band - near + k, half))
    if early:
        left = assemble(out_ref[pl.ds(near, half)], sign[band // half][:1])
        group = 4

        def synth(c, _):
            cols = pl.multiple_of(c * (group * BLK), 128)
            value = jnp.dot(
                left,
                table_part(table, near, half, pl.ds(cols, group * BLK)),
                preferred_element_type=F32,
            )
            partial[:, pl.ds(cols, group * BLK)] = value[: 2 * BLK]
            partial[:, pl.ds(cols + HALF_LON, group * BLK)] = value[2 * BLK :]
            return 0

        lax.fori_loop(0, XH // group, synth, 0, unroll=XH // group)
    build(3)

    def done(k, _):
        arrived(far + k)
        return 0

    def sent(i, _):
        copy_b(i).wait_send()
        return 0

    lax.fori_loop(0, half, done, 0)
    lax.fori_loop(1, nb, sent, 0)


def exchange(temp, surf, legendre, m_order, hydro, coupling, idx, wgt, nb, nl, early):
    _, lev_dev, _, width = temp.shape
    lat = legendre.shape[1]
    blocks = idx.shape[0]
    vmem = pl.BlockSpec(memory_space=pltpu.VMEM)
    hbm = pl.BlockSpec(memory_space=pltpu.HBM)
    out_shape = [
        jax.ShapeDtypeStruct((nb, 2 * PR, BLK), BF),
        jax.ShapeDtypeStruct((blocks // 2, 2 * HALF, 2 * BLK), BF),
    ]
    if early:
        out_shape.append(jax.ShapeDtypeStruct((nb * PR, HALF_LON), BF))
        out_shape.append(jax.ShapeDtypeStruct((2 * BLK, NLON), F32))
        out_shape.append(jax.ShapeDtypeStruct((2, 8, nb // 2 * PR), F32))
    return pl.pallas_call(
        functools.partial(exchange_kernel, nb, nl, lat, lev_dev, early),
        out_shape=out_shape,
        in_specs=[hbm] * 8,
        out_specs=[vmem] * len(out_shape),
        scratch_shapes=[
            pltpu.VMEM((S, lev_dev + 2, 2, width), BF),
            pltpu.VMEM(legendre.shape, BF),
            pltpu.VMEM(hydro.shape, BF),
            pltpu.VMEM(coupling.shape, F32),
            pltpu.VMEM(idx.shape, jnp.int32),
            pltpu.VMEM(wgt.shape, F32),
            pltpu.SMEM(m_order.shape, jnp.int32),
            pltpu.VMEM((BLOCKS + len(CHUNKS), Q * lat, BLK), F32),
            pltpu.VMEM((nl, len(CHUNKS) * Q * lat, BLK), BF),
            pltpu.VMEM((nl, S * lat, BLK), BF),
            pltpu.VMEM((3, nl * BLK, 2 * BLK), BF),
            pltpu.VMEM((nb + 2 if lat > 16 else 1, PR, 2 * BLK), F32),
            pltpu.VMEM((nb, 2 * PR, BLK), BF),
            pltpu.VMEM((nb * PR, BLK), F32),
            pltpu.SemaphoreType.DMA((2 * len(CHUNKS),)),
            pltpu.SemaphoreType.DMA((7,)),
            pltpu.SemaphoreType.DMA((len(CHUNKS) * nl,)),
            pltpu.SemaphoreType.DMA((len(CHUNKS) * nl,)),
            pltpu.SemaphoreType.DMA((nb,)),
            pltpu.SemaphoreType.DMA((nb,)),
        ],
        compiler_params=pltpu.CompilerParams(
            collective_id=0, has_side_effects=True, vmem_limit_bytes=(30 if early else 52) * 1024 * 1024
        ),
    )(*[
        pltpu.with_memory_space_constraint(x, pltpu.HBM)
        for x in (temp, surf, legendre, m_order, hydro, coupling, idx, wgt)
    ])


def grid_kernel(nb, lev_dev, early, src_ref, coef_ref, spread, *refs):
    if early:
        table, partial, sign, out_ref, src, pool, grid, ss, so = refs
    else:
        m_ref, out_ref, src, pool, grid, ss, so, table, signs = refs
        build_table(m_ref, table, signs, nb)
    load_src = pltpu.make_async_copy(src_ref, src, ss)
    load_src.start()
    band = lax.axis_index("band")
    half, _, far = halves(band, nb)
    if early:
        left = assemble(coef_ref[pl.ds(far, half)], sign[far // half][:1])
    else:
        left = assemble(coef_ref[...], signs[...].T[:1])
    group = 4

    def synth(c, _):
        cols = pl.multiple_of(c * (group * BLK), 128)
        part = pl.ds(cols, group * BLK)
        part = table_part(table, far, half, part) if early else table[:, part]
        both = jnp.dot(left, part, preferred_element_type=F32)
        for side in range(2):
            value = both[side * 2 * BLK : (side + 1) * 2 * BLK]
            if early:
                value = value + partial[:, pl.ds(cols + side * HALF_LON, group * BLK)]
            value = value.astype(BF)
            for t in range(3):
                for p in range(2):
                    at = p * BLK + t * KP
                    for g in range(group):
                        pool[(2 * t + p) * XB + side * XH + c * group + g, :KP] = value[
                            at : at + KP, g * BLK : (g + 1) * BLK
                        ]
        return 0

    lax.fori_loop(0, XH // group, synth, 0, unroll=XH // group if early else 1)
    load_src.wait()

    first = (band - 1) * (2 * XB)

    def read(x):
        source = jnp.concatenate(
            [
                jnp.concatenate([pool[src[i, j * XB + x] - first] for i in range(4)], axis=1)
                for j in range(2)
            ],
            axis=0,
        )
        return jnp.dot(source, spread[x], preferred_element_type=F32)

    def write(q):
        start = sum(PARTS[:q]) * BLK
        cols = pl.ds(start, PARTS[q] * BLK)
        return pltpu.make_async_copy(grid.at[:, :, cols], out_ref.at[:, :, cols], so.at[q])

    for q in range(len(PARTS)):
        for x in range(sum(PARTS[:q]), sum(PARTS[: q + 1])):
            value = read(x)
            for j in range(2):
                grid[:, j, x * BLK : (x + 1) * BLK] = value[
                    j * KS : j * KS + lev_dev, j * BLK : (j + 1) * BLK
                ]
        write(q).start()
    for q in range(len(PARTS)):
        write(q).wait()


def grid_part(src, m_order, coef, spread, table, nb, lev_dev):
    vmem = pl.BlockSpec(memory_space=pltpu.VMEM)
    hbm = pl.BlockSpec(memory_space=pltpu.HBM)
    early = len(table) > 0
    scratch = [
        pltpu.SMEM(src.shape, jnp.int32),
        pltpu.VMEM((JJ * XB, KS, BLK), BF),
        pltpu.VMEM((lev_dev, 2, NLON), F32),
        pltpu.SemaphoreType.DMA,
        pltpu.SemaphoreType.DMA((len(PARTS),)),
    ]
    src = pltpu.with_memory_space_constraint(src, pltpu.HBM)
    if early:
        last, specs = list(table), [vmem] * len(table)
    else:
        last, specs = [m_order], [pl.BlockSpec(memory_space=pltpu.SMEM)]
        scratch.append(pltpu.VMEM((nb * PR, HALF_LON), BF))
        scratch.append(pltpu.VMEM((nb * PR, BLK), F32))
    return pl.pallas_call(
        functools.partial(grid_kernel, nb, lev_dev, early),
        out_shape=jax.ShapeDtypeStruct((lev_dev, 2, NLON), F32),
        in_specs=[hbm, vmem, vmem] + specs,
        out_specs=hbm,
        scratch_shapes=scratch,
        compiler_params=pltpu.CompilerParams(
            vmem_limit_bytes=(24 if early else 54) * 1024 * 1024
        ),
    )(src, coef, spread, *last)


def shards(
    temp_spectrum,
    surf_spectrum,
    legendre,
    m_order,
    hydro_matrix,
    surf_coupling,
    src_blocks,
    tap_index,
    tap_weight,
):
    lev_dev = temp_spectrum.shape[3]
    nb, nl = lax.axis_size("band"), lax.axis_size("lev")
    early = nb <= 16
    coef, spread, *table = exchange(
        jnp.transpose(temp_spectrum, (0, 3, 2, 1)),
        jnp.transpose(surf_spectrum, (0, 2, 1)),
        legendre,
        m_order,
        hydro_matrix,
        surf_coupling[None, :],
        tap_index,
        tap_weight,
        nb,
        nl,
        early,
    )
    out = grid_part(src_blocks.T, m_order, coef, spread, table, nb, lev_dev)
    return jnp.transpose(out, (1, 0, 2))


def solution(mesh):
    in_specs = (
        P("band", None, None, "lev"),
        P("band", None, None),
        P("band", None, None),
        P(),
        P("lev", None),
        P("lev"),
        P("band", None),
        P("band", None, None),
        P("band", None, None),
    )
    out_specs = P("band", "lev", None)
    return jax.shard_map(shards, mesh=mesh, in_specs=in_specs, out_specs=out_specs, check_vma=False)
```

```python
import functools
import math

import jax
import jax.numpy as jnp
from jax import lax
from jax.experimental import pallas as pl
from jax.experimental.pallas import tpu as pltpu
from jax.sharding import PartitionSpec as P

NLON = 5120
BLK = 128
TAPS = 4
XB = NLON // BLK
XH = XB // 2
HALF_LON = NLON // 2
S = 20
CHUNKS = ((0, 8), (8, 8), (16, 4))
Q = 4
BLOCKS = S // Q
KP = 40
PR = 40
JJ = 6
HALF = 256
WORK = (5, 20, 15, 0)
KS = 48
PARTS = (14, 14, 8, 4)
MESH = pl.DeviceIdType.MESH
BF = jnp.bfloat16
F32 = jnp.float32


def iota(shape, dim):
    return lax.broadcasted_iota(jnp.int32, shape, dim)


def cosine(steps):
    steps = steps - NLON * jnp.floor(steps * (1.0 / NLON))
    y = (jnp.abs(steps * (1.0 / NLON) - 0.5) - 0.25) * (2.0 * math.pi)
    z = y * y
    p = -1.0 / 39916800.0
    for c in (1.0 / 362880.0, -1.0 / 5040.0, 1.0 / 120.0, -1.0 / 6.0, 1.0):
        p = p * z + c
    return y * p


def table_rows(m_ref, table, signs, pair):
    row = iota((8, BLK), 0)
    point = iota((8, BLK), 1).astype(F32)
    first, second, turns, parity = [], [], [], []
    for u in range(2):
        base = (pair * 2 + u) * S
        orders = []
        for start, count in CHUNKS:
            tile = jnp.zeros((8, BLK), F32)
            for i in range(8):
                value = m_ref[base + start + i % count].astype(F32)
                tile = jnp.where(row == i, value, tile)
            orders.append(tile)
        turn = [2.0 * cosine(o * float(BLK)) for o in orders]
        shift = jnp.where(row >= 4, NLON // 4, 0).astype(F32)
        for c, s in ((0, 0.0), (1, 0.0), (0, NLON / 4), (1, NLON / 4), (2, shift)):
            factor = jnp.where(orders[c] == 0.0, 1.0, 2.0)
            first.append(factor * cosine(orders[c] * point + s))
            second.append(factor * cosine(orders[c] * (point + float(BLK)) + s))
            turns.append(turn[c])
            half = orders[c] * 0.5
            parity.append(1.0 - 4.0 * (half - jnp.floor(half)))
    old = jnp.concatenate(first, axis=0)
    new = jnp.concatenate(second, axis=0)
    turn = jnp.concatenate(turns, axis=0)
    place = pl.ds(pl.multiple_of(pair * 2 * PR, 16), 2 * PR)
    signs[place, :] = jnp.concatenate(parity, axis=0)
    for x in range(XH):
        table[place, x * BLK : (x + 1) * BLK] = old.astype(BF)
        old, new = new, turn * new - old


def build_table(m_ref, table, signs, nb):
    def pair(b, _):
        table_rows(m_ref, table, signs, b)
        return 0

    lax.fori_loop(0, nb // 2, pair, 0)


def build_spread(idx, wgt, spread, first, last):
    cells = iota((HALF, BLK), 0).astype(BF)
    zero = jnp.zeros((HALF, BLK), BF)

    def block(x, _):
        for j in range(2):
            index = idx[j * XB + x]
            weight = wgt[j * XB + x].astype(BF)
            for h in range(2):
                spot = (index - h * HALF).astype(F32).astype(BF)
                total = None
                for t in range(TAPS):
                    hit = cells == jnp.broadcast_to(spot[t : t + 1, :], (HALF, BLK))
                    part = jnp.where(
                        hit, jnp.broadcast_to(weight[t : t + 1, :], (HALF, BLK)), zero
                    )
                    total = part if total is None else total + part
                spread[x, h * HALF : (h + 1) * HALF, j * BLK : (j + 1) * BLK] = total
        return 0

    lax.fori_loop(first, last, block, 0)


def assemble(coef, sign):
    left = []
    for p in range(2):
        tiles = []
        for b in range(coef.shape[0]):
            value = coef[b].astype(F32)
            for r, k in [(r, k) for r in range(2) for k in range(4)] + [(0, 4), (1, 4)]:
                at = r * PR + k * 2 * Q + p * Q
                tiles.append(value[at : at + Q])
        left.append(jnp.concatenate(tiles, axis=0).T)
    left = jnp.concatenate(left, axis=0)
    return jnp.concatenate([left, left * sign], axis=0).astype(BF)


def halves(band, nb):
    half = nb // 2
    near = (band // half) * half
    return half, near, lax.rem(near + half, nb)


def table_part(table, start, half, cols):
    return table[pl.ds(pl.multiple_of(start * PR, 16), half * PR), cols]


def exchange_kernel(
    nb, nl, lat, lev_dev, early, *refs
):
    (temp_ref, surf_ref, leg_ref, ord_ref, h_ref, c_ref, idx_ref, wgt_ref), refs = refs[:8], refs[8:]
    out_ref, spread = refs[:2]
    if early:
        table, partial, sign = refs[2:5]
    refs = refs[2 + 3 * early :]
    (buf, leg, h, coup, idx, wgt, m_ref, rows, gall, full, wide, total, pieces, signs) = refs[:14]
    (sl, sm, sa, ra, sb, rb) = refs[14:]
    band = lax.axis_index("band")
    lev = lax.axis_index("lev")
    chunks = len(CHUNKS)

    def load_temp(c):
        part = pl.ds(*CHUNKS[c])
        return pltpu.make_async_copy(temp_ref.at[part], buf.at[part, pl.ds(0, lev_dev)], sl.at[c])

    def load_leg(c):
        part = pl.ds(*CHUNKS[c])
        return pltpu.make_async_copy(leg_ref.at[part], leg.at[part], sl.at[chunks + c])

    load_surf = pltpu.make_async_copy(surf_ref, buf.at[:, lev_dev], sm.at[0])
    load_again = pltpu.make_async_copy(surf_ref, buf.at[:, lev_dev + 1], sm.at[6])
    load_h = pltpu.make_async_copy(h_ref, h, sm.at[1])
    load_c = pltpu.make_async_copy(c_ref, coup, sm.at[2])
    load_idx = pltpu.make_async_copy(idx_ref, idx, sm.at[3])
    load_wgt = pltpu.make_async_copy(wgt_ref, wgt, sm.at[4])
    load_m = pltpu.make_async_copy(ord_ref, m_ref, sm.at[5])
    load_idx.start()
    load_wgt.start()
    load_m.start()
    load_surf.start()
    load_again.start()
    load_leg(0).start()
    load_temp(0).start()

    barrier = pltpu.get_barrier_semaphore()

    def greet_lev(i, _):
        pl.semaphore_signal(
            barrier, inc=1, device_id=(band, lax.rem(lev + i, nl)), device_id_type=MESH
        )
        return 0

    def greet_band(i, _):
        pl.semaphore_signal(
            barrier, inc=1, device_id=(lax.rem(band + i, nb), lev), device_id_type=MESH
        )
        return 0

    lax.fori_loop(1, nb, greet_band, 0)
    lax.fori_loop(1, nl, greet_lev, 0)
    for c in range(1, chunks):
        load_leg(c).start()
        load_temp(c).start()
    load_h.start()
    load_c.start()
    load_idx.wait()
    load_wgt.wait()
    marks = [0]
    for count in WORK:
        marks.append(marks[-1] + count)
    assert 2 * marks[-1] == idx.shape[0]

    def build(part):
        build_spread(idx, wgt, spread, marks[part], marks[part + 1])

    build(0)

    def copy_a(i, c):
        part = pl.ds(c * Q * lat, Q * lat)
        return pltpu.make_async_remote_copy(
            src_ref=gall.at[lev, part],
            dst_ref=gall.at[lev, part],
            send_sem=sa.at[c * nl + i],
            recv_sem=ra.at[c * nl + i],
            device_id=(band, lax.rem(lev + i, nl)),
            device_id_type=MESH,
        )

    width = leg_ref.shape[2]
    used = 2 * lev_dev
    tail = 2 * used - BLK
    spare = used + 4
    order = iota((lat, width), 1)
    lane = iota((lat, BLK), 1)
    blank = jnp.zeros((lat, BLK - used - 4), F32)

    def transform(s):
        m = m_ref[band * S + s]
        keep = jnp.where(order >= m, 1.0, 0.0).astype(BF)
        coef = buf[s].reshape(used + 4, width)
        four = lax.dot_general(
            leg[s] * keep, coef, (((1,), (1,)), ((), ())), preferred_element_type=F32
        )
        return jnp.concatenate([four, blank], axis=1)

    def place(block, q, value):
        rows[block, pl.ds(q, lat, stride=Q), :] = value

    load_m.wait()
    load_surf.wait()
    load_again.wait()
    ends = [None] * Q
    for c, (start, count) in enumerate(CHUNKS):
        load_leg(c).wait()
        load_temp(c).wait()
        for q in range(Q):
            one = transform(start + q)
            place(start // Q, q, one)
            if count == 2 * Q:
                two = transform(start + Q + q)
                place(start // Q + 1, q, two)
                place(BLOCKS + c, q, jnp.where(lane < used, one, pltpu.roll(two, used, 1)))
                end = pltpu.roll(two, spare + c * tail - used + tail, 1)
                ends[q] = end if c == 0 else jnp.where(lane < spare + c * tail, ends[q], end)
            else:
                place(BLOCKS + c, q, jnp.where(lane < used, one, ends[q]))
        gall[lev, c * Q * lat : (c + 1) * Q * lat, :] = rows[BLOCKS + c].astype(BF)
        if c == 0:
            pl.semaphore_wait(barrier, nl - 1 + nb - 1)
        for i in range(1, nl):
            copy_a(i, c).start()
    for k in range(BLOCKS):
        full[lev, k * Q * lat : (k + 1) * Q * lat, :] = rows[k].astype(BF)

    depth = nl * BLK
    lev_total = h_ref.shape[1]
    load_h.wait()
    load_c.wait()
    row = iota((lev_dev, lev_total), 0) + lev * lev_dev
    col = iota((lev_dev, lev_total), 1)
    upper = jnp.where(col >= row, h[...].astype(F32), 0.0).astype(BF)
    row = iota((depth, lev_total), 0)
    col = iota((depth, lev_total), 1)
    spots = jnp.zeros((depth, lev_total), F32)
    for v in range(nl):
        step = row - v * BLK - 2 * (col - v * lev_dev)
        inside = (col >= v * lev_dev) & (col < (v + 1) * lev_dev)
        spots = jnp.where(inside & (step >= 0) & (step < 2), 1.0, spots)
    tall = lax.dot_general(
        spots.astype(BF), upper, (((1,), (1,)), ((), ())), preferred_element_type=F32
    )
    row = iota((depth, lev_dev), 0)
    mine = lev * BLK + 2 * lev_dev
    high = coup[...].astype(BF).astype(F32)
    tall = jnp.where(
        (row == mine) | (row == mine + 1), jnp.broadcast_to(high, (depth, lev_dev)), tall
    )
    tall = jnp.where(
        (row == mine + 2) | (row == mine + 3),
        jnp.broadcast_to(coup[...] - high, (depth, lev_dev)),
        tall,
    )
    tall = tall.astype(BF)
    row = iota((lev_dev, 2 * BLK), 0)
    col = iota((lev_dev, 2 * BLK), 1)
    odd = iota((depth, 2 * BLK), 0) & 1
    right = (iota((depth, 2 * BLK), 1) >= BLK).astype(jnp.int32)
    for t in range(3):
        onto = jnp.where((col & (BLK - 1)) == row + t * KP, 1.0, 0.0).astype(BF)
        spread_out = jnp.dot(tall, onto, preferred_element_type=F32)
        wide[t] = jnp.where(odd == right, spread_out, 0.0).astype(BF)

    build(1)

    for c in range(len(CHUNKS)):
        for i in range(1, nl):
            copy_a(i, c).wait()
    size = Q * lat
    lane = iota((size, BLK), 1)
    for i in range(1, nl):
        v = lax.rem(lev + i, nl)
        last = gall[v, 2 * size : 3 * size, :]
        full[v, 4 * size : 5 * size, :] = last
        last = last.astype(F32)
        for c in range(2):
            pair = gall[v, c * size : (c + 1) * size, :]
            full[v, 2 * c * size : (2 * c + 1) * size, :] = pair
            end = pltpu.roll(last, 2 * BLK + used - tail - spare - c * tail - BLK, 1)
            pair = jnp.where(lane < used - tail, pltpu.roll(pair.astype(F32), BLK - used, 1), end)
            full[v, (2 * c + 1) * size : (2 * c + 2) * size, :] = pair.astype(BF)

    group = 16
    pairs = group // 2

    def hydro(g):
        parts = []
        for k in range(BLOCKS):
            at = k * Q * lat + g * Q * group
            at = at if isinstance(at, int) else pl.multiple_of(at, 16)
            parts.append(pl.ds(at, Q * group))
        left = jnp.concatenate(
            [jnp.concatenate([full[v, p] for v in range(nl)], axis=1) for p in parts], axis=0
        )
        result = []
        for t in range(3):
            value = jnp.dot(left, wide[t], preferred_element_type=F32)
            value = value.reshape(BLOCKS, pairs, 2 * Q, 2 * BLK)
            result.append([value[:, p].reshape(PR, 2 * BLK) for p in range(pairs)])
        return result

    def pack(b, value):
        value = jnp.concatenate([value[:, :BLK], value[:, BLK:]], axis=0)
        pieces[b] = value.astype(BF)

    if lat == group:
        result = hydro(0)
        for b in range(nb):
            value = result[1][b]
            for t in (0, 2):
                if 0 <= b - 1 + t < pairs:
                    value = value + result[t][b - 1 + t]
            pack(b, value)
    else:
        total[...] = jnp.zeros_like(total)

        def many(g, _):
            result = hydro(g)
            for t in range(3):
                for p in range(pairs):
                    place = g * pairs + p + 2 - t
                    total[place] = total[place] + result[t][p]
            return 0

        def finish(b, _):
            pack(b, total[b + 1])
            return 0

        lax.fori_loop(0, lat // group, many, 0)
        lax.fori_loop(0, nb, finish, 0)

    def copy_b(i):
        peer = lax.rem(band + i, nb)
        return pltpu.make_async_remote_copy(
            src_ref=pieces.at[peer],
            dst_ref=out_ref.at[band],
            send_sem=sb.at[i],
            recv_sem=rb.at[i],
            device_id=(peer, lev),
            device_id_type=MESH,
        )

    half, near, far = halves(band, nb)

    def send(peer):
        copy_b(lax.rem(peer - band + nb, nb)).start()

    def send_far(k, _):
        send(far + jnp.where(far > 0, half - 1 - k, k))
        return 0

    def send_near(k, _):
        send(near + lax.rem(band - near + k, half))
        return 0

    lax.fori_loop(0, half, send_far, 0)
    lax.fori_loop(1, half, send_near, 0)
    out_ref[band] = pieces[band]
    def arrived(peer):
        copy_b(lax.rem(band - peer + nb, nb)).wait_recv()

    if early:
        build_table(m_ref, table, signs, nb)
        for k in range(2):
            sign[k] = signs[k * half * PR : (k + 1) * half * PR, :].T[:8]
    build(2)
    for k in range(1, half):
        arrived(near + lax.rem(band - near + k, half))
    if early:
        left = assemble(out_ref[pl.ds(near, half)], sign[band // half][:1])
        group = 4

        def synth(c, _):
            cols = pl.multiple_of(c * (group * BLK), 128)
            value = jnp.dot(
                left,
                table_part(table, near, half, pl.ds(cols, group * BLK)),
                preferred_element_type=F32,
            )
            partial[:, pl.ds(cols, group * BLK)] = value[: 2 * BLK]
            partial[:, pl.ds(cols + HALF_LON, group * BLK)] = value[2 * BLK :]
            return 0

        lax.fori_loop(0, XH // group, synth, 0, unroll=XH // group)
    build(3)

    def done(k, _):
        arrived(far + k)
        return 0

    def sent(i, _):
        copy_b(i).wait_send()
        return 0

    lax.fori_loop(0, half, done, 0)
    lax.fori_loop(1, nb, sent, 0)


def exchange(temp, surf, legendre, m_order, hydro, coupling, idx, wgt, nb, nl, early):
    _, lev_dev, _, width = temp.shape
    lat = legendre.shape[1]
    blocks = idx.shape[0]
    vmem = pl.BlockSpec(memory_space=pltpu.VMEM)
    hbm = pl.BlockSpec(memory_space=pltpu.HBM)
    out_shape = [
        jax.ShapeDtypeStruct((nb, 2 * PR, BLK), BF),
        jax.ShapeDtypeStruct((blocks // 2, 2 * HALF, 2 * BLK), BF),
    ]
    if early:
        out_shape.append(jax.ShapeDtypeStruct((nb * PR, HALF_LON), BF))
        out_shape.append(jax.ShapeDtypeStruct((2 * BLK, NLON), F32))
        out_shape.append(jax.ShapeDtypeStruct((2, 8, nb // 2 * PR), F32))
    return pl.pallas_call(
        functools.partial(exchange_kernel, nb, nl, lat, lev_dev, early),
        out_shape=out_shape,
        in_specs=[hbm] * 8,
        out_specs=[vmem] * len(out_shape),
        scratch_shapes=[
            pltpu.VMEM((S, lev_dev + 2, 2, width), BF),
            pltpu.VMEM(legendre.shape, BF),
            pltpu.VMEM(hydro.shape, BF),
            pltpu.VMEM(coupling.shape, F32),
            pltpu.VMEM(idx.shape, jnp.int32),
            pltpu.VMEM(wgt.shape, F32),
            pltpu.SMEM(m_order.shape, jnp.int32),
            pltpu.VMEM((BLOCKS + len(CHUNKS), Q * lat, BLK), F32),
            pltpu.VMEM((nl, len(CHUNKS) * Q * lat, BLK), BF),
            pltpu.VMEM((nl, S * lat, BLK), BF),
            pltpu.VMEM((3, nl * BLK, 2 * BLK), BF),
            pltpu.VMEM((nb + 2 if lat > 16 else 1, PR, 2 * BLK), F32),
            pltpu.VMEM((nb, 2 * PR, BLK), BF),
            pltpu.VMEM((nb * PR, BLK), F32),
            pltpu.SemaphoreType.DMA((2 * len(CHUNKS),)),
            pltpu.SemaphoreType.DMA((7,)),
            pltpu.SemaphoreType.DMA((len(CHUNKS) * nl,)),
            pltpu.SemaphoreType.DMA((len(CHUNKS) * nl,)),
            pltpu.SemaphoreType.DMA((nb,)),
            pltpu.SemaphoreType.DMA((nb,)),
        ],
        compiler_params=pltpu.CompilerParams(
            collective_id=0, has_side_effects=True, vmem_limit_bytes=(30 if early else 52) * 1024 * 1024
        ),
    )(*[
        pltpu.with_memory_space_constraint(x, pltpu.HBM)
        for x in (temp, surf, legendre, m_order, hydro, coupling, idx, wgt)
    ])


def grid_kernel(nb, lev_dev, early, src_ref, coef_ref, spread, *refs):
    if early:
        table, partial, sign, out_ref, src, pool, grid, ss, so = refs
    else:
        m_ref, out_ref, src, pool, grid, ss, so, table, signs = refs
        build_table(m_ref, table, signs, nb)
    load_src = pltpu.make_async_copy(src_ref, src, ss)
    load_src.start()
    band = lax.axis_index("band")
    half, _, far = halves(band, nb)
    if early:
        left = assemble(coef_ref[pl.ds(far, half)], sign[far // half][:1])
    else:
        left = assemble(coef_ref[...], signs[...].T[:1])
    group = 4

    def synth(c, _):
        cols = pl.multiple_of(c * (group * BLK), 128)
        part = pl.ds(cols, group * BLK)
        part = table_part(table, far, half, part) if early else table[:, part]
        both = jnp.dot(left, part, preferred_element_type=F32)
        for side in range(2):
            value = both[side * 2 * BLK : (side + 1) * 2 * BLK]
            if early:
                value = value + partial[:, pl.ds(cols + side * HALF_LON, group * BLK)]
            for t in range(3):
                for p in range(2):
                    at = p * BLK + t * KP
                    for g in range(group):
                        pool[(2 * t + p) * XB + side * XH + c * group + g] = value[
                            at : at + KS, g * BLK : (g + 1) * BLK
                        ].astype(BF)
        return 0

    lax.fori_loop(0, XH // group, synth, 0, unroll=XH // group if early else 1)
    load_src.wait()

    first = (band - 1) * (2 * XB)

    def read(x):
        source = jnp.concatenate(
            [
                jnp.concatenate([pool[src[i, j * XB + x] - first] for i in range(4)], axis=1)
                for j in range(2)
            ],
            axis=0,
        )
        return jnp.dot(source, spread[x], preferred_element_type=F32)

    def write(q):
        start = sum(PARTS[:q]) * BLK
        cols = pl.ds(start, PARTS[q] * BLK)
        return pltpu.make_async_copy(grid.at[:, :, cols], out_ref.at[:, :, cols], so.at[q])

    for q in range(len(PARTS)):
        for x in range(sum(PARTS[:q]), sum(PARTS[: q + 1])):
            value = read(x)
            for j in range(2):
                grid[:, j, x * BLK : (x + 1) * BLK] = value[
                    j * KS : j * KS + lev_dev, j * BLK : (j + 1) * BLK
                ]
        write(q).start()
    for q in range(len(PARTS)):
        write(q).wait()


def grid_part(src, m_order, coef, spread, table, nb, lev_dev):
    vmem = pl.BlockSpec(memory_space=pltpu.VMEM)
    hbm = pl.BlockSpec(memory_space=pltpu.HBM)
    early = len(table) > 0
    scratch = [
        pltpu.SMEM(src.shape, jnp.int32),
        pltpu.VMEM((JJ * XB, KS, BLK), BF),
        pltpu.VMEM((lev_dev, 2, NLON), F32),
        pltpu.SemaphoreType.DMA,
        pltpu.SemaphoreType.DMA((len(PARTS),)),
    ]
    src = pltpu.with_memory_space_constraint(src, pltpu.HBM)
    if early:
        last, specs = list(table), [vmem] * len(table)
    else:
        last, specs = [m_order], [pl.BlockSpec(memory_space=pltpu.SMEM)]
        scratch.append(pltpu.VMEM((nb * PR, HALF_LON), BF))
        scratch.append(pltpu.VMEM((nb * PR, BLK), F32))
    return pl.pallas_call(
        functools.partial(grid_kernel, nb, lev_dev, early),
        out_shape=jax.ShapeDtypeStruct((lev_dev, 2, NLON), F32),
        in_specs=[hbm, vmem, vmem] + specs,
        out_specs=hbm,
        scratch_shapes=scratch,
        compiler_params=pltpu.CompilerParams(
            vmem_limit_bytes=(24 if early else 54) * 1024 * 1024
        ),
    )(src, coef, spread, *last)


def shards(
    temp_spectrum,
    surf_spectrum,
    legendre,
    m_order,
    hydro_matrix,
    surf_coupling,
    src_blocks,
    tap_index,
    tap_weight,
):
    lev_dev = temp_spectrum.shape[3]
    nb, nl = lax.axis_size("band"), lax.axis_size("lev")
    early = nb <= 16
    coef, spread, *table = exchange(
        jnp.transpose(temp_spectrum, (0, 3, 2, 1)),
        jnp.transpose(surf_spectrum, (0, 2, 1)),
        legendre,
        m_order,
        hydro_matrix,
        surf_coupling[None, :],
        tap_index,
        tap_weight,
        nb,
        nl,
        early,
    )
    out = grid_part(src_blocks.T, m_order, coef, spread, table, nb, lev_dev)
    return jnp.transpose(out, (1, 0, 2))


def solution(mesh):
    in_specs = (
        P("band", None, None, "lev"),
        P("band", None, None),
        P("band", None, None),
        P(),
        P("lev", None),
        P("lev"),
        P("band", None),
        P("band", None, None),
        P("band", None, None),
    )
    out_specs = P("band", "lev", None)
    return jax.shard_map(shards, mesh=mesh, in_specs=in_specs, out_specs=out_specs, check_vma=False)
```
